512 devices in a mesh: group: 16 (over y, core), ctx: 32 (over z, x).
Axes of the slice: x: 4, y: 8, z: 8, core: 2. Of those that a mesh axis runs over, the one named last changes fastest.
Arguments:
- queries: bfloat16 [65536, 1024], P(('group', 'ctx')), may hold values from -8 to 8
- keys: bfloat16 [65536, 1024], P(('group', 'ctx')), may hold values from -6 to 6
- values: bfloat16 [65536, 1024], P(('group', 'ctx')), may hold values from -6 to 6
- cotangent: bfloat16 [65536, 1024], P(('group', 'ctx')), may hold values from -192 to 192
Outputs:
- output: bfloat16 [65536, 1024], P(('group', 'ctx'))
- grad_queries: bfloat16 [65536, 1024], P(('group', 'ctx'))
- grad_keys: bfloat16 [65536, 1024], P(('group', 'ctx'))
- grad_values: bfloat16 [65536, 1024], P(('group', 'ctx'))
The draws below stay inside these ranges and needn't reach their ends.
All inputs are finite; a program needn't handle non-finite values.
Results may differ from the reference program's by a relative error of at most 0.0096.
Values may be sent and summed in bfloat16 or wider, within the bound.
No kernel may reach another device: no remote copies, remote signals or barrier semaphores. Data moves between devices by JAX's collectives and lax.ppermute only.
A program may use at most 128 MiB of HBM per device.

```python
import math
import jax
import jax.numpy as jnp
from jax import lax

HEADS = 8
HEAD_DIM = 128
BLOCK = 128
COARSE_ONE = 16
COARSE_TWO = 16
TOK_DEV = 128
FEATURES = 1024
TOKENS = 65536
GROUP_ROWS = 256
LEVEL_ONE = 4096
LEVEL_TWO = 256
N_GROUP = 16
N_CTX = 32


def draw_queries(key, part):
    key = jax.random.fold_in(key, 11)
    first_key = jax.random.fold_in(key, 0)
    shape = (TOKENS, HEADS * HEAD_DIM)
    return jnp.clip(2.0 * jax.random.normal(first_key, shape, jnp.float32), -8.0, 8.0).astype(jnp.bfloat16)


def draw_keys(key, part):
    key = jax.random.fold_in(key, 12)
    shape = (TOKENS, HEADS * HEAD_DIM)
    return jnp.clip(jax.random.normal(key, shape, jnp.float32), -6.0, 6.0).astype(jnp.bfloat16)


def block_scale(key, dims, cuts, least, high):
    gain, own = 1.0, jax.random.fold_in(key, 6)
    for dim, blocks in cuts:
        draws = jnp.exp(jax.random.uniform(jax.random.fold_in(own, dim), (blocks,), jnp.float32, least / len(cuts), high / len(cuts)))
        gain = gain * jnp.repeat(draws, dims[dim] // blocks).reshape([-1 if axis == dim else 1 for axis in range(len(dims))])
    return gain


def scatter_about(own_key, dims, scale, limit, shards=(), kind=jnp.bfloat16):
    values = jax.random.normal(own_key, dims, jnp.float32) * scale
    if len(shards) > 0:
        values = block_scale(own_key, dims, shards, -0.22, 0.18) * values
    return jnp.clip(values, min=-limit, max=limit).astype(kind)


def setup_inputs(seed: int = 0) -> dict:
    key_of = jax.random.split(jax.random.key(seed), 5)
    return {
        "queries": draw_queries(jax.random.fold_in(key_of[4], 71), 0),
        "keys": draw_keys(jax.random.fold_in(key_of[4], 71), 0),
        "values": scatter_about(key_of[2], (TOKENS, FEATURES), 1.0, 6.0, ((0, 512),)),
        "cotangent": scatter_about(key_of[3], (TOKENS, FEATURES), 32.0, 192.0, ((0, 512),)),
    }


def attend(queries, cotangent, key_rows, value_rows, allowed):
    row_count = queries.shape[0]
    key_count = key_rows.shape[0]
    factor = HEAD_DIM ** (-0.5)
    query_h = queries.astype(jnp.float32).reshape(row_count, HEADS, HEAD_DIM)
    cot_h = cotangent.astype(jnp.float32).reshape(row_count, HEADS, HEAD_DIM)
    key_h = key_rows.astype(jnp.float32).reshape(key_count, HEADS, HEAD_DIM)
    value_h = value_rows.astype(jnp.float32).reshape(key_count, HEADS, HEAD_DIM)
    scores = jnp.einsum('rhd,nhd->hrn', query_h, key_h) * factor
    masked = jnp.where(allowed[None], scores, -jnp.inf)
    highest = lax.optimization_barrier(jnp.max(masked, axis=2, keepdims=True))
    weights = jnp.where(allowed[None], jnp.exp(scores - highest), 0.0)
    totals = lax.optimization_barrier(jnp.sum(weights, axis=2, keepdims=True))
    chance = weights / totals
    chance_low = chance.astype(jnp.bfloat16).astype(jnp.float32)
    blended = jnp.einsum('hrn,nhd->rhd', chance_low, value_h)
    output = blended.reshape(row_count, -1).astype(jnp.bfloat16)
    slopes = jnp.einsum('rhd,nhd->hrn', cot_h, value_h)
    centre = lax.optimization_barrier(jnp.sum(chance * slopes, axis=2, keepdims=True))
    dscore = (chance * (slopes - centre) * factor).astype(jnp.bfloat16).astype(jnp.float32)
    grad_q = jnp.einsum('hrn,nhd->rhd', dscore, key_h).reshape(row_count, -1).astype(jnp.bfloat16)
    grad_k = jnp.einsum('hrn,rhd->nhd', dscore, query_h).reshape(key_count, -1)
    grad_v = jnp.einsum('hrn,rhd->nhd', chance_low, cot_h).reshape(key_count, -1)
    return (output, grad_q, grad_k, grad_v)

def key_mask(device, group_index, tok_rows, group_rows, level_rows, seq_total):
    query_pos = device * tok_rows + jnp.arange(tok_rows, dtype=jnp.int32)
    query_block = query_pos // BLOCK
    window_pos = device * tok_rows - BLOCK + jnp.arange(tok_rows + 2 * BLOCK, dtype=jnp.int32)
    inside = (window_pos >= 0) & (window_pos < seq_total)
    near_field = inside[None, :] & (jnp.abs(window_pos[None, :] // BLOCK - query_block[:, None]) <= 1)
    coarse_pos = group_index * group_rows + jnp.arange(group_rows, dtype=jnp.int32)
    coarse_block = coarse_pos * COARSE_ONE // BLOCK
    first_level = jnp.abs(coarse_block[None, :] - query_block[:, None]) > 1
    level_group = jnp.arange(level_rows, dtype=jnp.int32) // (group_rows // COARSE_TWO)
    second_level = jnp.broadcast_to((level_group != group_index)[None, :], (tok_rows, level_rows))
    return jnp.concatenate([near_field, first_level, second_level], axis=1)

def reference(queries, keys, values, cotangent):
    devices_all = N_GROUP * N_CTX
    features = HEADS * HEAD_DIM
    key_value = jnp.stack([keys, values])
    level_one = (lax.optimization_barrier(jnp.sum(key_value.astype(jnp.float32).reshape(2, LEVEL_ONE, COARSE_ONE, features), axis=2)) / math.sqrt(COARSE_ONE)).astype(jnp.bfloat16)
    level_two = (lax.optimization_barrier(jnp.sum(level_one.astype(jnp.float32).reshape(2, LEVEL_TWO, COARSE_TWO, features), axis=2)) / math.sqrt(COARSE_TWO)).astype(jnp.bfloat16)
    padded = jnp.pad(key_value, ((0, 0), (BLOCK, BLOCK), (0, 0)))
    width = TOK_DEV + 2 * BLOCK

    def advance(running, device):
        fine_grad, grad_one, grad_two = running
        offset = (device * TOK_DEV).astype(jnp.int32)
        group_index = (device // N_CTX).astype(jnp.int32)
        query_rows = lax.dynamic_slice_in_dim(queries, offset, TOK_DEV, 0)
        cot_rows = lax.dynamic_slice_in_dim(cotangent, offset, TOK_DEV, 0)
        window = lax.dynamic_slice_in_dim(padded, offset, width, 1)
        group_start = (group_index * GROUP_ROWS).astype(jnp.int32)
        group_level = lax.dynamic_slice_in_dim(level_one, group_start, GROUP_ROWS, 1)
        allkeys = jnp.concatenate([window, group_level, level_two], axis=1)
        allowed = key_mask(device, group_index, TOK_DEV, GROUP_ROWS, LEVEL_TWO, TOKENS)
        output, grad_q, grad_k, grad_v = attend(query_rows, cot_rows, allkeys[0], allkeys[1], allowed)
        grads = jnp.stack([grad_k, grad_v])
        previous = lax.dynamic_slice_in_dim(fine_grad, offset, width, 1)
        fine_grad = lax.dynamic_update_slice_in_dim(fine_grad, previous + grads[:, :width], offset, 1)
        before_one = lax.dynamic_slice_in_dim(grad_one, group_start, GROUP_ROWS, 1)
        grad_one = lax.dynamic_update_slice_in_dim(grad_one, before_one + grads[:, width:width + GROUP_ROWS], group_start, 1)
        grad_two = grad_two + grads[:, width + GROUP_ROWS:]
        return ((fine_grad, grad_one, grad_two), (output, grad_q))
    start_state = (jnp.zeros((2, TOKENS + 2 * BLOCK, features), jnp.float32), jnp.zeros((2, LEVEL_ONE, features), jnp.float32), jnp.zeros((2, LEVEL_TWO, features), jnp.float32))
    final_state, pieces = lax.scan(advance, start_state, jnp.arange(devices_all, dtype=jnp.int32))
    fine_grad, grad_one, grad_two = final_state
    output = pieces[0].reshape(TOKENS, features)
    grad_queries = pieces[1].reshape(TOKENS, features)
    carried_one = grad_one + jnp.repeat(grad_two, COARSE_TWO, axis=1) / math.sqrt(COARSE_TWO)
    gradient = fine_grad[:, BLOCK:BLOCK + TOKENS] + jnp.repeat(carried_one, COARSE_ONE, axis=1) / math.sqrt(COARSE_ONE)
    return (output, grad_queries, gradient[0].astype(jnp.bfloat16), gradient[1].astype(jnp.bfloat16))
```

```python
import jax
import jax.numpy as jnp
from jax import lax
from jax.experimental import pallas as pl
from jax.experimental.pallas import tpu as pltpu
from jax.sharding import PartitionSpec as P

HEADS = 8
HEAD_DIM = 128
BLOCK = 128
COARSE = 16
ONE_ROWS = BLOCK // COARSE
N_CTX = 32
N_GROUP = 16
GROUP_ROWS = N_CTX * ONE_ROWS
TWO_ROWS = GROUP_ROWS // COARSE
LEVEL_TWO = N_GROUP * TWO_ROWS
FEATURES = HEADS * HEAD_DIM
FACTOR = HEAD_DIM ** (-0.5)
SHUT = -1e30
F32 = jnp.float32
BF16 = jnp.bfloat16
VMEM = pl.BlockSpec(memory_space=pltpu.VMEM)
SMEM = pl.BlockSpec(memory_space=pltpu.SMEM)


def shifted(value, steps):
    count = N_CTX * N_GROUP
    first, last = (max(0, -steps), min(count, count - steps))
    return lax.ppermute(value, ("group", "ctx"), [(s, s + steps) for s in range(first, last)])


def dot_nt(left, right):
    return lax.dot_general(left, right, (((1,), (1,)), ((), ())), preferred_element_type=F32)


def dot_nn(left, right):
    return lax.dot_general(left, right, (((1,), (0,)), ((), ())), preferred_element_type=F32)


def dot_tn(left, right):
    return lax.dot_general(left, right, (((0,), (0,)), ((), ())), preferred_element_type=F32)


def rows_of(shape, dim):
    return lax.broadcasted_iota(jnp.int32, shape, dim)


def coarsen_one_kernel(keys, values, spread):
    row, token = rows_of((2 * ONE_ROWS, BLOCK), 0), rows_of((2 * ONE_ROWS, BLOCK), 1)
    pick_k = jnp.where(row == token // COARSE, 1.0, 0.0).astype(BF16)
    pick_v = jnp.where(row - ONE_ROWS == token // COARSE, 1.0, 0.0).astype(BF16)
    own = (dot_nn(pick_k, keys[...]) + dot_nn(pick_v, values[...])) * 0.25
    own = own.astype(BF16)
    for copy in range(N_CTX):
        spread[copy] = own


def coarsen_two_kernel(level_one, spread):
    total = N_CTX * 2 * ONE_ROWS
    row, source = rows_of((2 * TWO_ROWS, total), 0), rows_of((2 * TWO_ROWS, total), 1)
    kind = (source % (2 * ONE_ROWS)) // ONE_ROWS
    pick = jnp.where(row == kind * TWO_ROWS + source // (4 * ONE_ROWS), 1.0, 0.0).astype(BF16)
    own = (dot_nn(pick, level_one[...].reshape(total, FEATURES)) * 0.25).astype(BF16)
    for copy in range(N_GROUP):
        spread[copy] = own


def split_one(block):
    wide = block.astype(F32)
    key = wide[:, :ONE_ROWS].reshape(GROUP_ROWS, HEAD_DIM).astype(BF16)
    value = wide[:, ONE_ROWS:].reshape(GROUP_ROWS, HEAD_DIM).astype(BF16)
    return key, value


def near_bias(place):
    group, ctx = place[0], place[1]
    device = group * N_CTX + ctx
    low = jnp.where(device == 0, SHUT, 0.0).astype(F32)
    high = jnp.where(device == N_CTX * N_GROUP - 1, SHUT, 0.0).astype(F32)
    shape = (BLOCK, HEAD_DIM)
    row = rows_of((GROUP_ROWS, HEAD_DIM), 0) // ONE_ROWS
    one = jnp.where(jnp.abs(row - ctx) <= 1, SHUT, 0.0).astype(F32)
    return [jnp.full(shape, low), jnp.zeros(shape, F32), jnp.full(shape, high), one]


def two_bias(place):
    row = rows_of((LEVEL_TWO, HEAD_DIM), 0) // TWO_ROWS
    return jnp.where(row == place[0], SHUT, 0.0).astype(F32)


def stats_kernel(place, queries, cotangent, keys, values, below, above, level_one, stats, bias):
    @pl.when(pl.program_id(0) == 0)
    def _():
        bias[...] = jnp.concatenate(near_bias(place), axis=0)

    one_k, one_v = split_one(level_one[...])
    all_k = jnp.concatenate([below[:BLOCK], keys[...], above[:BLOCK], one_k], axis=0)
    all_v = jnp.concatenate([below[BLOCK:], values[...], above[BLOCK:], one_v], axis=0)
    scores = dot_nt(all_k, queries[...]) * FACTOR + bias[...]
    highest = jnp.max(scores, axis=0, keepdims=True)
    weights = jnp.exp(scores - highest)
    slopes = dot_nt(all_v, cotangent[...])
    total = jnp.sum(weights, axis=0, keepdims=True)
    centre = jnp.sum(weights * slopes, axis=0, keepdims=True)
    stats[0, 0:1] = highest
    stats[0, 1:2] = total
    stats[0, 2:3] = centre


def two_kernel(place, queries, cotangent, level_two, near, stats, part_two):
    bias = two_bias(place)
    for head in range(HEADS):
        lanes = slice(head * HEAD_DIM, (head + 1) * HEAD_DIM)
        query, cot = queries[:, lanes], cotangent[:, lanes]
        key = level_two[:, :TWO_ROWS, lanes].reshape(LEVEL_TWO, HEAD_DIM)
        value = level_two[:, TWO_ROWS:, lanes].reshape(LEVEL_TWO, HEAD_DIM)
        scores = dot_nt(key, query) * FACTOR + bias
        slopes = dot_nt(value, cot)
        near_highest = near[head, 0:1]
        highest = jnp.maximum(near_highest, jnp.max(scores, axis=0, keepdims=True))
        scale = jnp.exp(near_highest - highest)
        weights = jnp.exp(scores - highest)
        total = near[head, 1:2] * scale + jnp.sum(weights, axis=0, keepdims=True)
        inverse = 1.0 / total
        centre = near[head, 2:3] * scale + jnp.sum(weights * slopes, axis=0, keepdims=True)
        centre = centre * inverse
        stats[head, 0:1] = highest
        stats[head, 1:2] = inverse
        stats[head, 2:3] = centre
        chance = weights * inverse
        dscore = (chance * (slopes - centre) * FACTOR).astype(BF16)
        grad_k = dot_nn(dscore, query).reshape(N_GROUP, TWO_ROWS, HEAD_DIM)
        grad_v = dot_nn(chance.astype(BF16), cot).reshape(N_GROUP, TWO_ROWS, HEAD_DIM)
        part_two[:, :, lanes] = jnp.concatenate([grad_k, grad_v], axis=1).astype(BF16)


def attend_kernel(
    place, queries, cotangent, keys, values, below, above, level_one, level_two, stats,
    output, grad_q, fine, grad_below, grad_above, part_one, bias,
):
    @pl.when(pl.program_id(0) == 0)
    def _():
        bias[...] = jnp.concatenate(near_bias(place) + [two_bias(place)], axis=0)

    query, cot = queries[...], cotangent[...]
    one_k, one_v = split_one(level_one[...])
    two_k = level_two[:, :TWO_ROWS].reshape(LEVEL_TWO, HEAD_DIM)
    two_v = level_two[:, TWO_ROWS:].reshape(LEVEL_TWO, HEAD_DIM)
    all_k = jnp.concatenate([below[:BLOCK], keys[...], above[:BLOCK], one_k, two_k], axis=0)
    all_v = jnp.concatenate([below[BLOCK:], values[...], above[BLOCK:], one_v, two_v], axis=0)
    scores = dot_nt(all_k, query) * FACTOR + bias[...]
    chance = jnp.exp(scores - stats[0, 0:1]) * stats[0, 1:2]
    slopes = dot_nt(all_v, cot)
    dscore = (chance * (slopes - stats[0, 2:3]) * FACTOR).astype(BF16)
    chance = chance.astype(BF16)
    output[...] = dot_tn(chance, all_v).astype(BF16)
    grad_q[...] = dot_tn(dscore, all_k).astype(BF16)
    seen = 3 * BLOCK + GROUP_ROWS
    grad_k = dot_nn(dscore[:seen], query)
    grad_v = dot_nn(chance[:seen], cot)
    grad_below[:BLOCK] = grad_k[:BLOCK].astype(BF16)
    grad_below[BLOCK:] = grad_v[:BLOCK].astype(BF16)
    fine[:BLOCK] = grad_k[BLOCK : 2 * BLOCK]
    fine[BLOCK:] = grad_v[BLOCK : 2 * BLOCK]
    grad_above[:BLOCK] = grad_k[2 * BLOCK : 3 * BLOCK].astype(BF16)
    grad_above[BLOCK:] = grad_v[2 * BLOCK : 3 * BLOCK].astype(BF16)
    one_k = grad_k[3 * BLOCK :].reshape(N_CTX, ONE_ROWS, HEAD_DIM)
    one_v = grad_v[3 * BLOCK :].reshape(N_CTX, ONE_ROWS, HEAD_DIM)
    part_one[...] = jnp.concatenate([one_k, one_v], axis=1)


def merge_kernel(part_one, arrived, merged):
    for head in range(HEADS):
        lanes = slice(head * HEAD_DIM, (head + 1) * HEAD_DIM)
        two = jnp.sum(arrived[:, :, lanes].astype(F32), axis=0) * 0.25
        for ctx in range(N_CTX):
            low, high = ctx // 2, TWO_ROWS + ctx // 2
            carried = jnp.concatenate(
                [
                    jnp.broadcast_to(two[low : low + 1], (ONE_ROWS, HEAD_DIM)),
                    jnp.broadcast_to(two[high : high + 1], (ONE_ROWS, HEAD_DIM)),
                ],
                axis=0,
            )
            merged[ctx, :, lanes] = (part_one[ctx, :, lanes] + carried).astype(BF16)


def finish_kernel(fine, from_below, from_above, arrived, grad_keys, grad_values):
    for head in range(HEADS):
        lanes = slice(head * HEAD_DIM, (head + 1) * HEAD_DIM)
        owned = jnp.sum(arrived[:, :, lanes].astype(F32), axis=0) * 0.25
        for first, out in ((0, grad_keys), (1, grad_values)):
            rows = slice(first * BLOCK, (first + 1) * BLOCK)
            total = fine[rows, lanes] + from_below[rows, lanes].astype(F32)
            total = total + from_above[rows, lanes].astype(F32)
            carried = owned[first * ONE_ROWS : (first + 1) * ONE_ROWS].reshape(ONE_ROWS, 1, HEAD_DIM)
            total = total.reshape(ONE_ROWS, COARSE, HEAD_DIM) + carried
            out[:, lanes] = total.reshape(BLOCK, HEAD_DIM).astype(BF16)


def shape_of(shape, dtype):
    return jax.ShapeDtypeStruct(shape, dtype)


def per_head(*shape):
    block = shape + (HEAD_DIM,)
    lead = (0,) * len(shape)
    return pl.BlockSpec(block, lambda head: lead + (head,))


def local(queries, keys, values, cotangent):
    group_index = lax.axis_index("group")
    ctx_index = lax.axis_index("ctx")
    place = jnp.stack([group_index, ctx_index]).astype(jnp.int32)
    one_shape = (N_CTX, 2 * ONE_ROWS, FEATURES)
    two_shape = (N_GROUP, 2 * TWO_ROWS, FEATURES)

    spread_one = pl.pallas_call(
        coarsen_one_kernel,
        out_shape=shape_of(one_shape, BF16),
        in_specs=[VMEM] * 2,
        out_specs=VMEM,
        name="coarsen_one",
    )(keys, values)
    level_one = lax.all_to_all(spread_one, "ctx", 0, 0, tiled=True)
    pair = jnp.concatenate([keys, values], axis=0)
    below = shifted(pair, 1)
    above = shifted(pair, -1)
    spread_two = pl.pallas_call(
        coarsen_two_kernel,
        out_shape=shape_of(two_shape, BF16),
        in_specs=[VMEM],
        out_specs=VMEM,
        name="coarsen_two",
    )(level_one)
    level_two = lax.all_to_all(spread_two, "group", 0, 0, tiled=True)

    stats_shape = shape_of((HEADS, 8, HEAD_DIM), F32)
    stats_spec = pl.BlockSpec((1, 8, HEAD_DIM), lambda head: (head, 0, 0))
    tok, both = per_head(BLOCK), per_head(2 * BLOCK)
    near = pl.pallas_call(
        stats_kernel,
        grid=(HEADS,),
        out_shape=stats_shape,
        in_specs=[SMEM, tok, tok, tok, tok, both, both, per_head(*one_shape[:2])],
        out_specs=stats_spec,
        scratch_shapes=[pltpu.VMEM((3 * BLOCK + GROUP_ROWS, HEAD_DIM), F32)],
        cost_estimate=pl.CostEstimate(
            flops=4 * BLOCK * 640 * FEATURES, bytes_accessed=4 << 20, transcendentals=640 * 1024
        ),
        name="near_stats",
    )(place, queries, cotangent, keys, values, below, above, level_one)

    stats, part_two = pl.pallas_call(
        two_kernel,
        out_shape=(stats_shape, shape_of(two_shape, BF16)),
        in_specs=[SMEM] + [VMEM] * 4,
        out_specs=(VMEM, VMEM),
        name="level_two",
    )(place, queries, cotangent, level_two, near)
    arrived_two = lax.all_to_all(part_two, "group", 0, 0, tiled=True)

    output, grad_q, fine, grad_below, grad_above, part_one = pl.pallas_call(
        attend_kernel,
        grid=(HEADS,),
        out_shape=(
            shape_of((BLOCK, FEATURES), BF16),
            shape_of((BLOCK, FEATURES), BF16),
            shape_of((2 * BLOCK, FEATURES), F32),
            shape_of((2 * BLOCK, FEATURES), BF16),
            shape_of((2 * BLOCK, FEATURES), BF16),
            shape_of(one_shape, F32),
        ),
        in_specs=[SMEM, tok, tok, tok, tok, both, both, per_head(*one_shape[:2])]
        + [per_head(*two_shape[:2]), stats_spec],
        out_specs=(tok, tok, both, both, both, per_head(*one_shape[:2])),
        scratch_shapes=[pltpu.VMEM((3 * BLOCK + GROUP_ROWS + LEVEL_TWO, HEAD_DIM), F32)],
        cost_estimate=pl.CostEstimate(
            flops=12 * BLOCK * 896 * FEATURES, bytes_accessed=10 << 20, transcendentals=896 * 1024
        ),
        name="attend",
    )(place, queries, cotangent, keys, values, below, above, level_one, level_two, stats)

    from_above = shifted(grad_below, -1)
    from_below = shifted(grad_above, 1)
    merged = pl.pallas_call(
        merge_kernel,
        out_shape=shape_of(one_shape, BF16),
        in_specs=[VMEM] * 2,
        out_specs=VMEM,
        name="merge",
    )(part_one, arrived_two)
    arrived_one = lax.all_to_all(merged, "ctx", 0, 0, tiled=True)
    grad_keys, grad_values = pl.pallas_call(
        finish_kernel,
        out_shape=(shape_of((BLOCK, FEATURES), BF16),) * 2,
        in_specs=[VMEM] * 4,
        out_specs=(VMEM, VMEM),
        name="finish",
    )(fine, from_below, from_above, arrived_one)
    return (output, grad_q, grad_keys, grad_values)


def solution(mesh):
    placed = P(("group", "ctx"), None)
    return jax.shard_map(
        local,
        mesh=mesh,
        in_specs=(placed,) * 4,
        out_specs=(placed,) * 4,
        check_vma=False,
    )
```

```python
import jax
import jax.numpy as jnp
from jax import lax
from jax.experimental import pallas as pl
from jax.experimental.pallas import tpu as pltpu
from jax.sharding import Mesh
from jax.sharding import PartitionSpec as P

HEADS = 8
HEAD_DIM = 128
BLOCK = 128
COARSE = 16
ONE_ROWS = BLOCK // COARSE
N_Y, N_CORE, N_Z, N_X = 8, 2, 8, 4
AXES = ("y", "core", "z", "x")
ROW = ("core", "x")
N_BLOCK = N_CORE * N_X
N_CTX = N_Z * N_X
N_GROUP = N_Y * N_CORE
GROUP_ROWS = N_CTX * ONE_ROWS
TWO_ROWS = GROUP_ROWS // COARSE
LEVEL_TWO = N_GROUP * TWO_ROWS
FEATURES = HEADS * HEAD_DIM
FACTOR = HEAD_DIM ** (-0.5)
SHUT = -1e30
F32 = jnp.float32
BF16 = jnp.bfloat16
VMEM = pl.BlockSpec(memory_space=pltpu.VMEM)
SMEM = pl.BlockSpec(memory_space=pltpu.SMEM)
QUERY, KEY, VALUE, COT = (slice(i * BLOCK, (i + 1) * BLOCK) for i in range(4))
PAIR = slice(BLOCK, 3 * BLOCK)


def dot_nt(left, right):
    return lax.dot_general(left, right, (((1,), (1,)), ((), ())), preferred_element_type=F32)


def dot_nn(left, right):
    return lax.dot_general(left, right, (((1,), (0,)), ((), ())), preferred_element_type=F32)


def dot_tn(left, right):
    return lax.dot_general(left, right, (((0,), (0,)), ((), ())), preferred_element_type=F32)


def iota(shape, dim):
    return lax.broadcasted_iota(jnp.int32, shape, dim)


def lanes_of(head):
    return slice(head * HEAD_DIM, (head + 1) * HEAD_DIM)


def pack_kernel(queries, keys, values, cotangent, packed):
    for head in range(HEADS):
        for rows, source in ((QUERY, queries), (KEY, keys), (VALUE, values), (COT, cotangent)):
            packed[head, rows] = source[:, lanes_of(head)]


def coarsen_one_kernel(held, spread):
    row, token = iota((2 * ONE_ROWS, BLOCK), 0), iota((2 * ONE_ROWS, BLOCK), 1)
    pick_k = jnp.where(row == token // COARSE, 1.0, 0.0).astype(BF16)
    pick_v = jnp.where(row - ONE_ROWS == token // COARSE, 1.0, 0.0).astype(BF16)
    pick = jnp.concatenate([pick_k, pick_v], axis=1)
    for block in range(N_BLOCK):
        own = (dot_nn(pick, held[block, PAIR]) * 0.25).astype(BF16)
        rows = slice(block * 2 * ONE_ROWS, (block + 1) * 2 * ONE_ROWS)
        for copy in range(N_Z):
            spread[copy, rows] = own


def coarsen_two_kernel(level_one, spread):
    width = N_BLOCK * 2 * ONE_ROWS
    shape = (N_CORE * 2 * TWO_ROWS, N_Z * width)
    row, source = iota(shape, 0), iota(shape, 1)
    z, rest = source // width, source % width
    group, rest = rest // (width // 2), rest % (width // 2)
    x, kind = rest // (2 * ONE_ROWS), (rest % (2 * ONE_ROWS)) // ONE_ROWS
    target = (group * 2 + kind) * TWO_ROWS + (z * N_X + x) // 2
    pick = jnp.where(row == target, 1.0, 0.0).astype(BF16)
    own = dot_nn(pick, level_one[...].reshape(N_Z * width, HEAD_DIM))
    own = (own * 0.25).astype(BF16)
    for copy in range(N_Y):
        spread[copy] = own


def split_one(level_one, group):
    half = N_X * 2 * ONE_ROWS
    wide = level_one[:, group * half : (group + 1) * half].astype(F32)
    wide = wide.reshape(N_CTX, 2 * ONE_ROWS, HEAD_DIM)
    key = wide[:, :ONE_ROWS].reshape(GROUP_ROWS, HEAD_DIM).astype(BF16)
    value = wide[:, ONE_ROWS:].reshape(GROUP_ROWS, HEAD_DIM).astype(BF16)
    return key, value


def near_bias(place, block):
    y, z = place[0], place[1]
    group, x = block // N_X, block % N_X
    shape = (BLOCK, HEAD_DIM)
    low, high = jnp.zeros(shape, F32), jnp.zeros(shape, F32)
    if block == 0:
        low = jnp.full(shape, jnp.where((y == 0) & (z == 0), SHUT, 0.0).astype(F32))
    if block == N_BLOCK - 1:
        high = jnp.full(shape, jnp.where((y == N_Y - 1) & (z == N_Z - 1), SHUT, 0.0).astype(F32))
    row = iota((GROUP_ROWS, HEAD_DIM), 0) // ONE_ROWS
    one = jnp.where(jnp.abs(row - (z * N_X + x)) <= 1, SHUT, 0.0).astype(F32)
    return [low, jnp.zeros(shape, F32), high, one]


def two_bias(place, group):
    row = iota((LEVEL_TWO, HEAD_DIM), 0) // TWO_ROWS
    return jnp.where(row == place[0] * N_CORE + group, SHUT, 0.0).astype(F32)


def near_window(held, below, above, block, first):
    group, x = block // N_X, block % N_X
    rows = slice(BLOCK + first * BLOCK, BLOCK + (first + 1) * BLOCK)
    halo = slice(first * BLOCK, (first + 1) * BLOCK)
    low = below[group, halo] if x == 0 else held[block - 1, rows]
    high = above[group, halo] if x == N_X - 1 else held[block + 1, rows]
    return [low, held[block, rows], high]


def near_kernel(place, held, below, above, level_one, stats):
    for group in range(N_CORE):
        one_k, one_v = split_one(level_one, group)
        for block in range(group * N_X, (group + 1) * N_X):
            all_k = jnp.concatenate(near_window(held, below, above, block, 0) + [one_k], axis=0)
            all_v = jnp.concatenate(near_window(held, below, above, block, 1) + [one_v], axis=0)
            bias = jnp.concatenate(near_bias(place, block), axis=0)
            scores = dot_nt(all_k, held[block, QUERY]) * FACTOR + bias
            highest = jnp.max(scores, axis=0, keepdims=True)
            weights = jnp.exp(scores - highest)
            slopes = dot_nt(all_v, held[block, COT])
            stats[block, 0:1] = highest
            stats[block, 1:2] = jnp.sum(weights, axis=0, keepdims=True)
            stats[block, 2:3] = jnp.sum(weights * slopes, axis=0, keepdims=True)


def two_kernel(place, held, level_two, near, stats, part_two, chances, dscores):
    key = level_two[:, :TWO_ROWS].reshape(LEVEL_TWO, HEAD_DIM)
    value = level_two[:, TWO_ROWS:].reshape(LEVEL_TWO, HEAD_DIM)
    for group in range(N_CORE):
        bias = two_bias(place, group)
        for block in range(group * N_X, (group + 1) * N_X):
            scores = dot_nt(key, held[block, QUERY]) * FACTOR + bias
            slopes = dot_nt(value, held[block, COT])
            near_highest = near[block, 0:1]
            highest = jnp.maximum(near_highest, jnp.max(scores, axis=0, keepdims=True))
            scale = jnp.exp(near_highest - highest)
            weights = jnp.exp(scores - highest)
            total = near[block, 1:2] * scale + jnp.sum(weights, axis=0, keepdims=True)
            inverse = 1.0 / total
            centre = near[block, 2:3] * scale + jnp.sum(weights * slopes, axis=0, keepdims=True)
            centre = centre * inverse
            stats[block, 0:1] = highest
            stats[block, 1:2] = inverse
            stats[block, 2:3] = centre
            chance = weights * inverse
            dscores[:, lanes_of(block)] = (chance * (slopes - centre) * FACTOR).astype(BF16)
            chances[:, lanes_of(block)] = chance.astype(BF16)
    tokens = N_BLOCK * BLOCK
    grad_k = dot_nn(dscores[...], held[:, QUERY].reshape(tokens, HEAD_DIM))
    grad_v = dot_nn(chances[...], held[:, COT].reshape(tokens, HEAD_DIM))
    grad_k = grad_k.reshape(N_GROUP, TWO_ROWS, HEAD_DIM)
    grad_v = grad_v.reshape(N_GROUP, TWO_ROWS, HEAD_DIM)
    part_two[...] = jnp.concatenate([grad_k, grad_v], axis=1).astype(BF16)


def attend_kernel(
    place, held, below, above, level_one, level_two, stats,
    answer, fine, grad_below, grad_above, part_one, window, ones,
):
    two_k = level_two[:, :TWO_ROWS].reshape(LEVEL_TWO, HEAD_DIM)
    two_v = level_two[:, TWO_ROWS:].reshape(LEVEL_TWO, HEAD_DIM)
    near = 3 * BLOCK
    seen = near + GROUP_ROWS
    for group in range(N_CORE):
        one_k, one_v = split_one(level_one, group)
        shut = two_bias(place, group)
        window[...] = jnp.zeros_like(window)
        for block in range(group * N_X, (group + 1) * N_X):
            x = block % N_X
            query, cot = held[block, QUERY], held[block, COT]
            near_k = near_window(held, below, above, block, 0)
            near_v = near_window(held, below, above, block, 1)
            all_k = jnp.concatenate(near_k + [one_k, two_k], axis=0)
            all_v = jnp.concatenate(near_v + [one_v, two_v], axis=0)
            bias = jnp.concatenate(near_bias(place, block) + [shut], axis=0)
            scores = dot_nt(all_k, query) * FACTOR + bias
            chance = jnp.exp(scores - stats[block, 0:1]) * stats[block, 1:2]
            slopes = dot_nt(all_v, cot)
            dscore = (chance * (slopes - stats[block, 2:3]) * FACTOR).astype(BF16)
            chance = chance.astype(BF16)
            answer[block, :BLOCK] = dot_tn(chance, all_v).astype(BF16)
            answer[block, BLOCK:] = dot_tn(dscore, all_k).astype(BF16)
            for kind, (left, right) in enumerate(((dscore, query), (chance, cot))):
                grad = dot_nn(left[:seen], right)
                window[kind, x * BLOCK : (x + 3) * BLOCK] += grad[:near]
                ones[kind] = grad[near:] if x == 0 else ones[kind] + grad[near:]
        for kind in range(2):
            rows = slice(kind * BLOCK, (kind + 1) * BLOCK)
            grad_below[group, rows] = window[kind, :BLOCK].astype(BF16)
            grad_above[group, rows] = window[kind, (N_X + 1) * BLOCK :].astype(BF16)
            for x in range(N_X):
                fine[group * N_X + x, rows] = window[kind, (x + 1) * BLOCK : (x + 2) * BLOCK]
        both = [ones[kind].reshape(N_CTX, ONE_ROWS, HEAD_DIM) for kind in range(2)]
        both = jnp.concatenate(both, axis=1).reshape(N_Z, N_X * 2 * ONE_ROWS, HEAD_DIM)
        half = N_X * 2 * ONE_ROWS
        part_one[:, group * half : (group + 1) * half] = both


def merge_kernel(part_one, arrived, merged):
    two = jnp.sum(arrived[...].astype(F32), axis=0) * 0.25
    for group in range(N_CORE):
        for ctx in range(N_CTX):
            z, x = ctx // N_X, ctx % N_X
            low = group * 2 * TWO_ROWS + ctx // 2
            high = low + TWO_ROWS
            first = (group * N_X + x) * 2 * ONE_ROWS
            rows = slice(first, first + 2 * ONE_ROWS)
            carried = jnp.concatenate(
                [
                    jnp.broadcast_to(two[low : low + 1], (ONE_ROWS, HEAD_DIM)),
                    jnp.broadcast_to(two[high : high + 1], (ONE_ROWS, HEAD_DIM)),
                ],
                axis=0,
            )
            merged[z, rows] = (part_one[z, rows] + carried).astype(BF16)


def finish_kernel(answer, fine, from_below, from_above, arrived, result):
    owned = jnp.sum(arrived[...].astype(F32), axis=0) * 0.25
    for block in range(N_BLOCK):
        group, x = block // N_X, block % N_X
        result[block, : 2 * BLOCK] = answer[block]
        for kind in range(2):
            rows = slice(kind * BLOCK, (kind + 1) * BLOCK)
            total = fine[block, rows]
            if x == 0:
                total = total + from_below[group, rows].astype(F32)
            if x == N_X - 1:
                total = total + from_above[group, rows].astype(F32)
            first = (2 * block + kind) * ONE_ROWS
            carried = owned[first : first + ONE_ROWS].reshape(ONE_ROWS, 1, HEAD_DIM)
            total = total.reshape(ONE_ROWS, COARSE, HEAD_DIM) + carried
            out = slice((2 + kind) * BLOCK, (3 + kind) * BLOCK)
            result[block, out] = total.reshape(BLOCK, HEAD_DIM).astype(BF16)


def unpack_kernel(packed, output, grad_q, grad_k, grad_v):
    for head in range(HEADS):
        for place, out in enumerate((output, grad_q, grad_k, grad_v)):
            out[:, lanes_of(head)] = packed[head, place * BLOCK : (place + 1) * BLOCK]


def shape_of(shape, dtype):
    return jax.ShapeDtypeStruct(shape, dtype)


def run(kernel, name, out_shape, *args, scratch=(), place=False, cost=None):
    several = isinstance(out_shape, tuple)
    specs = [SMEM if place and i == 0 else VMEM for i in range(len(args))]
    return pl.pallas_call(
        kernel,
        out_shape=out_shape,
        in_specs=specs,
        out_specs=(VMEM,) * len(out_shape) if several else VMEM,
        scratch_shapes=list(scratch),
        cost_estimate=cost,
        name=name,
    )(*args)


def at(y, z):
    return y * N_Z + z


SPOTS = [(y, z) for y in range(N_Y) for z in range(N_Z)]
RISE = (
    [(at(y, z), at(y, (z + 1) % N_Z)) for y, z in SPOTS],
    [(at(y, z), at(y, z) + 1) for y, z in SPOTS if at(y, z) + 1 < N_Y * N_Z],
)
FALL = (
    [(at(y, z), at(y, z) - 1) for y, z in SPOTS if at(y, z) > 0],
    [(at(y, z), at(y, (z - 1) % N_Z)) for y, z in SPOTS],
)


def exchange(parts, routes, swap):
    first, second = (lax.ppermute(v, ("y", "z"), r) for v, r in zip(parts, routes))
    return jnp.where(swap, jnp.stack([second, first]), jnp.stack([first, second]))


def local(queries, keys, values, cotangent):
    y, z = lax.axis_index("y"), lax.axis_index("z")
    place = jnp.stack([y, z]).astype(jnp.int32)
    wide = (HEADS, 4 * BLOCK, HEAD_DIM)
    one = (N_Z, N_BLOCK * 2 * ONE_ROWS, HEAD_DIM)
    two = (N_GROUP, 2 * TWO_ROWS, HEAD_DIM)
    halo = (N_CORE, 2 * BLOCK, HEAD_DIM)
    tokens = N_BLOCK * BLOCK

    packed = run(pack_kernel, "pack", shape_of(wide, BF16), queries, keys, values, cotangent)
    held = lax.all_to_all(packed, ROW, 0, 0, tiled=True)

    spread = run(coarsen_one_kernel, "coarsen_one", shape_of(one, BF16), held)
    level_one = lax.all_to_all(spread, "z", 0, 0, tiled=True)
    below = exchange([held[N_X - 1, PAIR], held[N_BLOCK - 1, PAIR]], RISE, z == 0)
    above = exchange([held[0, PAIR], held[N_X, PAIR]], FALL, z == N_Z - 1)

    spread = run(coarsen_two_kernel, "coarsen_two", shape_of((N_Y, 4 * TWO_ROWS, HEAD_DIM), BF16), level_one)
    level_two = lax.all_to_all(spread, "y", 0, 0, tiled=True).reshape(two)

    stats_shape = shape_of((N_BLOCK, 8, HEAD_DIM), F32)
    near = run(
        near_kernel, "near_stats", stats_shape, place, held, below, above, level_one, place=True,
        cost=pl.CostEstimate(
            flops=4 * tokens * 640 * HEAD_DIM, bytes_accessed=2 << 20, transcendentals=640 * tokens
        ),
    )
    stats, part_two = run(
        two_kernel, "level_two", (stats_shape, shape_of(two, BF16)),
        place, held, level_two, near, place=True,
        scratch=[pltpu.VMEM((LEVEL_TWO, tokens), BF16)] * 2,
    )
    part_two = part_two.reshape(N_Y, 4 * TWO_ROWS, HEAD_DIM)
    arrived_two = lax.all_to_all(part_two, "y", 0, 0, tiled=True)

    answer, fine, grad_below, grad_above, part_one = run(
        attend_kernel, "attend",
        (
            shape_of((N_BLOCK, 2 * BLOCK, HEAD_DIM), BF16),
            shape_of((N_BLOCK, 2 * BLOCK, HEAD_DIM), F32),
            shape_of(halo, BF16),
            shape_of(halo, BF16),
            shape_of(one, F32),
        ),
        place, held, below, above, level_one, level_two, stats, place=True,
        scratch=[
            pltpu.VMEM((2, (N_X + 2) * BLOCK, HEAD_DIM), F32),
            pltpu.VMEM((2, GROUP_ROWS, HEAD_DIM), F32),
        ],
        cost=pl.CostEstimate(
            flops=12 * tokens * 896 * HEAD_DIM, bytes_accessed=4 << 20, transcendentals=896 * tokens
        ),
    )
    from_below = exchange([grad_above[0], grad_above[1]], RISE, z == 0)
    from_above = exchange([grad_below[0], grad_below[1]], FALL, z == N_Z - 1)

    merged = run(merge_kernel, "merge", shape_of(one, BF16), part_one, arrived_two)
    arrived_one = lax.all_to_all(merged, "z", 0, 0, tiled=True)
    result = run(
        finish_kernel, "finish", shape_of(wide, BF16), answer, fine, from_below, from_above, arrived_one
    )
    arrived = lax.all_to_all(result, ROW, 0, 0, tiled=True)
    return run(unpack_kernel, "unpack", (shape_of((BLOCK, FEATURES), BF16),) * 4, arrived)


def solution(mesh):
    rows = Mesh(mesh.devices.reshape(N_Y, N_CORE, N_Z, N_X), AXES)
    placed = P(AXES, None)
    return jax.shard_map(
        local,
        mesh=rows,
        in_specs=(placed,) * 4,
        out_specs=(placed,) * 4,
        check_vma=False,
    )
```

```python
import jax
import jax.numpy as jnp
from jax import lax
from jax.experimental import pallas as pl
from jax.experimental.pallas import tpu as pltpu
from jax.sharding import Mesh
from jax.sharding import PartitionSpec as P

HEADS = 8
HEAD_DIM = 128
BLOCK = 128
COARSE = 16
ONE_ROWS = BLOCK // COARSE
N_Y, N_CORE, N_Z, N_X = 8, 2, 8, 4
AXES = ("y", "core", "z", "x")
GROUP = ("y", "core")
LINE = ("y", "core", "z")
N_HEAD = HEADS // N_X
N_UNIT = N_X * N_HEAD
N_CTX = N_Z * N_X
N_GROUP = N_Y * N_CORE
GROUP_ROWS = N_CTX * ONE_ROWS
TWO_ROWS = GROUP_ROWS // COARSE
LEVEL_TWO = N_GROUP * TWO_ROWS
FEATURES = HEADS * HEAD_DIM
FACTOR = HEAD_DIM ** (-0.5)
SHUT = -1e30
LIMIT = 24 << 20
F32 = jnp.float32
BF16 = jnp.bfloat16
VMEM = pl.BlockSpec(memory_space=pltpu.VMEM)
SMEM = pl.BlockSpec(memory_space=pltpu.SMEM)
QUERY, KEY, VALUE, COT = (slice(i * BLOCK, (i + 1) * BLOCK) for i in range(4))
PAIR = slice(BLOCK, 3 * BLOCK)


def dot_nt(left, right):
    return lax.dot_general(left, right, (((1,), (1,)), ((), ())), preferred_element_type=F32)


def dot_nn(left, right):
    return lax.dot_general(left, right, (((1,), (0,)), ((), ())), preferred_element_type=F32)


def dot_tn(left, right):
    return lax.dot_general(left, right, (((0,), (0,)), ((), ())), preferred_element_type=F32)


def iota(shape, dim):
    return lax.broadcasted_iota(jnp.int32, shape, dim)


def lanes_of(head):
    return slice(head * HEAD_DIM, (head + 1) * HEAD_DIM)


def pack_kernel(queries, keys, values, cotangent, packed):
    for head in range(HEADS):
        for rows, source in ((QUERY, queries), (KEY, keys), (VALUE, values), (COT, cotangent)):
            packed[head, rows] = source[:, lanes_of(head)]


def coarsen_one_kernel(held, spread):
    row, token = iota((2 * ONE_ROWS, BLOCK), 0), iota((2 * ONE_ROWS, BLOCK), 1)
    pick_k = jnp.where(row == token // COARSE, 1.0, 0.0).astype(BF16)
    pick_v = jnp.where(row - ONE_ROWS == token // COARSE, 1.0, 0.0).astype(BF16)
    pick = jnp.concatenate([pick_k, pick_v], axis=1)
    for unit in range(N_UNIT):
        own = (dot_nn(pick, held[unit, PAIR]) * 0.25).astype(BF16)
        rows = slice(unit * 2 * ONE_ROWS, (unit + 1) * 2 * ONE_ROWS)
        for copy in range(N_Z):
            spread[copy, rows] = own


def coarsen_two_kernel(level_one, spread):
    width = N_UNIT * 2 * ONE_ROWS
    shape = (N_HEAD * 2 * TWO_ROWS, N_Z * width)
    row, source = iota(shape, 0), iota(shape, 1)
    z, rest = source // width, source % width
    unit, kind = rest // (2 * ONE_ROWS), (rest % (2 * ONE_ROWS)) // ONE_ROWS
    x, head = unit // N_HEAD, unit % N_HEAD
    target = (head * 2 + kind) * TWO_ROWS + (z * N_X + x) // 2
    pick = jnp.where(row == target, 1.0, 0.0).astype(BF16)
    own = dot_nn(pick, level_one[...].reshape(N_Z * width, HEAD_DIM))
    own = (own * 0.25).astype(BF16)
    for copy in range(N_GROUP):
        spread[copy] = own


def split_one(level_one, head):
    wide = level_one[...].reshape(N_CTX, N_HEAD, 2 * ONE_ROWS, HEAD_DIM)[:, head].astype(F32)
    key = wide[:, :ONE_ROWS].reshape(GROUP_ROWS, HEAD_DIM).astype(BF16)
    value = wide[:, ONE_ROWS:].reshape(GROUP_ROWS, HEAD_DIM).astype(BF16)
    return key, value


def split_two(level_two, head):
    first = head * 2 * TWO_ROWS
    key = level_two[:, first : first + TWO_ROWS].reshape(LEVEL_TWO, HEAD_DIM)
    value = level_two[:, first + TWO_ROWS : first + 2 * TWO_ROWS].reshape(LEVEL_TWO, HEAD_DIM)
    return key, value


def near_bias(place, x):
    group, z = place[0], place[1]
    shape = (BLOCK, HEAD_DIM)
    low, high = jnp.zeros(shape, F32), jnp.zeros(shape, F32)
    if x == 0:
        low = jnp.full(shape, jnp.where((group == 0) & (z == 0), SHUT, 0.0).astype(F32))
    if x == N_X - 1:
        last = (group == N_GROUP - 1) & (z == N_Z - 1)
        high = jnp.full(shape, jnp.where(last, SHUT, 0.0).astype(F32))
    row = iota((GROUP_ROWS, HEAD_DIM), 0) // ONE_ROWS
    one = jnp.where(jnp.abs(row - (z * N_X + x)) <= 1, SHUT, 0.0).astype(F32)
    return [low, jnp.zeros(shape, F32), high, one]


def two_bias(place):
    row = iota((LEVEL_TWO, HEAD_DIM), 0) // TWO_ROWS
    return jnp.where(row == place[0], SHUT, 0.0).astype(F32)


def near_window(held, below, above, x, head, kind):
    rows = slice((1 + kind) * BLOCK, (2 + kind) * BLOCK)
    halo = slice(kind * BLOCK, (kind + 1) * BLOCK)
    unit = x * N_HEAD + head
    low = below[head, halo] if x == 0 else held[unit - N_HEAD, rows]
    high = above[head, halo] if x == N_X - 1 else held[unit + N_HEAD, rows]
    return [low, held[unit, rows], high]


def near_kernel(place, held, below, above, level_one, stats):
    for head in range(N_HEAD):
        one_k, one_v = split_one(level_one, head)
        for x in range(N_X):
            unit = x * N_HEAD + head
            all_k = jnp.concatenate(near_window(held, below, above, x, head, 0) + [one_k], axis=0)
            all_v = jnp.concatenate(near_window(held, below, above, x, head, 1) + [one_v], axis=0)
            bias = jnp.concatenate(near_bias(place, x), axis=0)
            scores = dot_nt(all_k, held[unit, QUERY]) * FACTOR + bias
            highest = jnp.max(scores, axis=0, keepdims=True)
            weights = jnp.exp(scores - highest)
            slopes = dot_nt(all_v, held[unit, COT])
            stats[unit, 0:1] = highest
            stats[unit, 1:2] = jnp.sum(weights, axis=0, keepdims=True)
            stats[unit, 2:3] = jnp.sum(weights * slopes, axis=0, keepdims=True)


def two_kernel(place, held, level_two, near, stats, part_two, chances, dscores):
    bias = two_bias(place)
    tokens = N_X * BLOCK
    for head in range(N_HEAD):
        key, value = split_two(level_two, head)
        for x in range(N_X):
            unit = x * N_HEAD + head
            scores = dot_nt(key, held[unit, QUERY]) * FACTOR + bias
            slopes = dot_nt(value, held[unit, COT])
            near_highest = near[unit, 0:1]
            highest = jnp.maximum(near_highest, jnp.max(scores, axis=0, keepdims=True))
            scale = jnp.exp(near_highest - highest)
            weights = jnp.exp(scores - highest)
            total = near[unit, 1:2] * scale + jnp.sum(weights, axis=0, keepdims=True)
            inverse = 1.0 / total
            centre = near[unit, 2:3] * scale + jnp.sum(weights * slopes, axis=0, keepdims=True)
            centre = centre * inverse
            stats[unit, 0:1] = highest
            stats[unit, 1:2] = inverse
            stats[unit, 2:3] = centre
            chance = weights * inverse
            dscores[head, :, lanes_of(x)] = (chance * (slopes - centre) * FACTOR).astype(BF16)
            chances[head, :, lanes_of(x)] = chance.astype(BF16)
        queries = jnp.concatenate([held[x * N_HEAD + head, QUERY] for x in range(N_X)], axis=0)
        cots = jnp.concatenate([held[x * N_HEAD + head, COT] for x in range(N_X)], axis=0)
        grad_k = dot_nn(dscores[head], queries).reshape(N_GROUP, TWO_ROWS, HEAD_DIM)
        grad_v = dot_nn(chances[head], cots).reshape(N_GROUP, TWO_ROWS, HEAD_DIM)
        rows = slice(head * 2 * TWO_ROWS, (head + 1) * 2 * TWO_ROWS)
        part_two[:, rows] = jnp.concatenate([grad_k, grad_v], axis=1).astype(BF16)


def attend_kernel(
    place, held, below, above, level_one, level_two, stats,
    answer, fine, grad_below, grad_above, part_one, window, ones,
):
    near = 3 * BLOCK
    seen = near + GROUP_ROWS
    shut = two_bias(place)
    for head in range(N_HEAD):
        one_k, one_v = split_one(level_one, head)
        two_k, two_v = split_two(level_two, head)
        window[head] = jnp.zeros_like(window[head])
        for x in range(N_X):
            unit = x * N_HEAD + head
            query, cot = held[unit, QUERY], held[unit, COT]
            near_k = near_window(held, below, above, x, head, 0)
            near_v = near_window(held, below, above, x, head, 1)
            all_k = jnp.concatenate(near_k + [one_k, two_k], axis=0)
            all_v = jnp.concatenate(near_v + [one_v, two_v], axis=0)
            bias = jnp.concatenate(near_bias(place, x) + [shut], axis=0)
            scores = dot_nt(all_k, query) * FACTOR + bias
            chance = jnp.exp(scores - stats[unit, 0:1]) * stats[unit, 1:2]
            slopes = dot_nt(all_v, cot)
            dscore = (chance * (slopes - stats[unit, 2:3]) * FACTOR).astype(BF16)
            chance = chance.astype(BF16)
            answer[unit, :BLOCK] = dot_tn(chance, all_v).astype(BF16)
            answer[unit, BLOCK:] = dot_tn(dscore, all_k).astype(BF16)
            for kind, (left, right) in enumerate(((dscore, query), (chance, cot))):
                grad = dot_nn(left[:seen], right)
                window[head, kind, x * BLOCK : (x + 3) * BLOCK] += grad[:near]
                ones[head, kind] = grad[near:] if x == 0 else ones[head, kind] + grad[near:]
        for kind in range(2):
            rows = slice(kind * BLOCK, (kind + 1) * BLOCK)
            grad_below[head, rows] = window[head, kind, :BLOCK].astype(BF16)
            grad_above[head, rows] = window[head, kind, (N_X + 1) * BLOCK :].astype(BF16)
            for x in range(N_X):
                fine[x * N_HEAD + head, rows] = window[head, kind, (x + 1) * BLOCK : (x + 2) * BLOCK]
        both = [ones[head, kind].reshape(N_CTX, ONE_ROWS, HEAD_DIM) for kind in range(2)]
        both = jnp.concatenate(both, axis=1)
        for ctx in range(N_CTX):
            first = ((ctx % N_X) * N_HEAD + head) * 2 * ONE_ROWS
            part_one[ctx // N_X, first : first + 2 * ONE_ROWS] = both[ctx]


def merge_kernel(part_one, arrived, merged):
    two = jnp.sum(arrived[...].astype(F32), axis=0) * 0.25
    for ctx in range(N_CTX):
        z, x = ctx // N_X, ctx % N_X
        for head in range(N_HEAD):
            low = head * 2 * TWO_ROWS + ctx // 2
            high = low + TWO_ROWS
            first = (x * N_HEAD + head) * 2 * ONE_ROWS
            rows = slice(first, first + 2 * ONE_ROWS)
            carried = jnp.concatenate(
                [
                    jnp.broadcast_to(two[low : low + 1], (ONE_ROWS, HEAD_DIM)),
                    jnp.broadcast_to(two[high : high + 1], (ONE_ROWS, HEAD_DIM)),
                ],
                axis=0,
            )
            merged[z, rows] = (part_one[z, rows] + carried).astype(BF16)


def finish_kernel(answer, fine, from_below, from_above, arrived, result):
    owned = jnp.sum(arrived[...].astype(F32), axis=0) * 0.25
    for unit in range(N_UNIT):
        x, head = unit // N_HEAD, unit % N_HEAD
        result[unit, : 2 * BLOCK] = answer[unit]
        for kind in range(2):
            rows = slice(kind * BLOCK, (kind + 1) * BLOCK)
            total = fine[unit, rows]
            if x == 0:
                total = total + from_below[head, rows].astype(F32)
            if x == N_X - 1:
                total = total + from_above[head, rows].astype(F32)
            first = (2 * unit + kind) * ONE_ROWS
            carried = owned[first : first + ONE_ROWS].reshape(ONE_ROWS, 1, HEAD_DIM)
            total = total.reshape(ONE_ROWS, COARSE, HEAD_DIM) + carried
            out = slice((2 + kind) * BLOCK, (3 + kind) * BLOCK)
            result[unit, out] = total.reshape(BLOCK, HEAD_DIM).astype(BF16)


def unpack_kernel(packed, output, grad_q, grad_k, grad_v):
    for head in range(HEADS):
        for place, out in enumerate((output, grad_q, grad_k, grad_v)):
            out[:, lanes_of(head)] = packed[head, place * BLOCK : (place + 1) * BLOCK]


def shape_of(shape, dtype):
    return jax.ShapeDtypeStruct(shape, dtype)


def run(kernel, name, out_shape, *args, scratch=(), place=False, cost=None):
    several = isinstance(out_shape, tuple)
    specs = [SMEM if place and i == 0 else VMEM for i in range(len(args))]
    return pl.pallas_call(
        kernel,
        out_shape=out_shape,
        in_specs=specs,
        out_specs=(VMEM,) * len(out_shape) if several else VMEM,
        scratch_shapes=list(scratch),
        compiler_params=pltpu.CompilerParams(vmem_limit_bytes=LIMIT),
        cost_estimate=cost,
        name=name,
    )(*args)


def shifted(value, steps):
    count = N_GROUP * N_Z
    first, last = max(0, -steps), min(count, count - steps)
    return lax.ppermute(value, LINE, [(s, s + steps) for s in range(first, last)])


def local(queries, keys, values, cotangent):
    group, z = lax.axis_index(GROUP), lax.axis_index("z")
    place = jnp.stack([group, z]).astype(jnp.int32)
    wide = (HEADS, 4 * BLOCK, HEAD_DIM)
    one = (N_Z, N_UNIT * 2 * ONE_ROWS, HEAD_DIM)
    two = (N_GROUP, N_HEAD * 2 * TWO_ROWS, HEAD_DIM)
    halo = (N_HEAD, 2 * BLOCK, HEAD_DIM)
    tokens = N_UNIT * BLOCK

    packed = run(pack_kernel, "pack", shape_of(wide, BF16), queries, keys, values, cotangent)
    held = lax.all_to_all(packed, "x", 0, 0, tiled=True)

    spread = run(coarsen_one_kernel, "coarsen_one", shape_of(one, BF16), held)
    level_one = lax.all_to_all(spread, "z", 0, 0, tiled=True)
    below = shifted(held[-N_HEAD:, PAIR], 1)
    above = shifted(held[:N_HEAD, PAIR], -1)

    spread = run(coarsen_two_kernel, "coarsen_two", shape_of(two, BF16), level_one)
    level_two = lax.all_to_all(spread, GROUP, 0, 0, tiled=True)

    stats_shape = shape_of((N_UNIT, 8, HEAD_DIM), F32)
    near = run(
        near_kernel, "near_stats", stats_shape, place, held, below, above, level_one, place=True,
        cost=pl.CostEstimate(
            flops=4 * tokens * 640 * HEAD_DIM, bytes_accessed=2 << 20, transcendentals=640 * tokens
        ),
    )
    stats, part_two = run(
        two_kernel, "level_two", (stats_shape, shape_of(two, BF16)),
        place, held, level_two, near, place=True,
        scratch=[pltpu.VMEM((N_HEAD, LEVEL_TWO, N_X * BLOCK), BF16)] * 2,
    )
    arrived_two = lax.all_to_all(part_two, GROUP, 0, 0, tiled=True)

    answer, fine, grad_below, grad_above, part_one = run(
        attend_kernel, "attend",
        (
            shape_of((N_UNIT, 2 * BLOCK, HEAD_DIM), BF16),
            shape_of((N_UNIT, 2 * BLOCK, HEAD_DIM), F32),
            shape_of(halo, BF16),
            shape_of(halo, BF16),
            shape_of(one, F32),
        ),
        place, held, below, above, level_one, level_two, stats, place=True,
        scratch=[
            pltpu.VMEM((N_HEAD, 2, (N_X + 2) * BLOCK, HEAD_DIM), F32),
            pltpu.VMEM((N_HEAD, 2, GROUP_ROWS, HEAD_DIM), F32),
        ],
        cost=pl.CostEstimate(
            flops=12 * tokens * 896 * HEAD_DIM, bytes_accessed=4 << 20, transcendentals=896 * tokens
        ),
    )
    merged = run(merge_kernel, "merge", shape_of(one, BF16), part_one, arrived_two)
    merged, grad_below, grad_above = lax.optimization_barrier((merged, grad_below, grad_above))
    arrived_one = lax.all_to_all(merged, "z", 0, 0, tiled=True)
    from_below = shifted(grad_above, 1)
    from_above = shifted(grad_below, -1)
    result = run(
        finish_kernel, "finish", shape_of(wide, BF16), answer, fine, from_below, from_above, arrived_one
    )
    arrived = lax.all_to_all(result, "x", 0, 0, tiled=True)
    return run(unpack_kernel, "unpack", (shape_of((BLOCK, FEATURES), BF16),) * 4, arrived)


def solution(mesh):
    rows = Mesh(mesh.devices.reshape(N_Y, N_CORE, N_Z, N_X), AXES)
    placed = P(AXES, None)
    return jax.shard_map(
        local,
        mesh=rows,
        in_specs=(placed,) * 4,
        out_specs=(placed,) * 4,
        check_vma=False,
    )
```

```python
import jax
import jax.numpy as jnp
from jax import lax
from jax.experimental import pallas as pl
from jax.experimental.pallas import tpu as pltpu
from jax.sharding import Mesh
from jax.sharding import PartitionSpec as P

HEADS = 8
HEAD_DIM = 128
BLOCK = 128
COARSE = 16
ONE_ROWS = BLOCK // COARSE
N_Y, N_CORE, N_Z, N_X = 8, 2, 8, 4
AXES = ("y", "core", "z", "x")
GROUP = ("y", "core")
LINE = ("y", "core", "z")
N_HEAD = HEADS // N_X
N_UNIT = N_X * N_HEAD
N_CTX = N_Z * N_X
N_GROUP = N_Y * N_CORE
GROUP_ROWS = N_CTX * ONE_ROWS
TWO_ROWS = GROUP_ROWS // COARSE
LEVEL_TWO = N_GROUP * TWO_ROWS
FEATURES = HEADS * HEAD_DIM
FACTOR = HEAD_DIM ** (-0.5)
SHUT = -1e30
PHASE = pl.CostEstimate(flops=60_000_000_000, bytes_accessed=200 << 20, transcendentals=0)
LIMIT = 6 << 20
F32 = jnp.float32
BF16 = jnp.bfloat16
VMEM = pl.BlockSpec(memory_space=pltpu.VMEM)
SMEM = pl.BlockSpec(memory_space=pltpu.SMEM)
QUERY, KEY, VALUE, COT = (slice(i * BLOCK, (i + 1) * BLOCK) for i in range(4))
PAIR = slice(BLOCK, 3 * BLOCK)


def dot_nt(left, right):
    return lax.dot_general(left, right, (((1,), (1,)), ((), ())), preferred_element_type=F32)


def dot_nn(left, right):
    return lax.dot_general(left, right, (((1,), (0,)), ((), ())), preferred_element_type=F32)


def dot_tn(left, right):
    return lax.dot_general(left, right, (((0,), (0,)), ((), ())), preferred_element_type=F32)


def iota(shape, dim):
    return lax.broadcasted_iota(jnp.int32, shape, dim)


def lanes_of(head):
    return slice(head * HEAD_DIM, (head + 1) * HEAD_DIM)


def pack_kernel(queries, keys, values, cotangent, packed):
    for head in range(HEADS):
        for rows, source in ((QUERY, queries), (KEY, keys), (VALUE, values), (COT, cotangent)):
            packed[head, rows] = source[:, lanes_of(head)]


def coarsen_one_kernel(held, spread):
    row, token = iota((2 * ONE_ROWS, BLOCK), 0), iota((2 * ONE_ROWS, BLOCK), 1)
    pick_k = jnp.where(row == token // COARSE, 1.0, 0.0).astype(BF16)
    pick_v = jnp.where(row - ONE_ROWS == token // COARSE, 1.0, 0.0).astype(BF16)
    pick = jnp.concatenate([pick_k, pick_v], axis=1)
    for unit in range(N_UNIT):
        own = (dot_nn(pick, held[unit, PAIR]) * 0.25).astype(BF16)
        rows = slice(unit * 2 * ONE_ROWS, (unit + 1) * 2 * ONE_ROWS)
        for copy in range(N_Z):
            spread[copy, rows] = own


def coarsen_two_kernel(level_one, spread):
    width = N_UNIT * 2 * ONE_ROWS
    shape = (N_HEAD * 2 * TWO_ROWS, N_Z * width)
    row, source = iota(shape, 0), iota(shape, 1)
    z, rest = source // width, source % width
    unit, kind = rest // (2 * ONE_ROWS), (rest % (2 * ONE_ROWS)) // ONE_ROWS
    x, head = unit // N_HEAD, unit % N_HEAD
    target = (head * 2 + kind) * TWO_ROWS + (z * N_X + x) // 2
    pick = jnp.where(row == target, 1.0, 0.0).astype(BF16)
    own = dot_nn(pick, level_one[...].reshape(N_Z * width, HEAD_DIM))
    own = (own * 0.25).astype(BF16)
    for copy in range(N_GROUP):
        spread[copy] = own


def split_one(level_one, head):
    wide = level_one[...].reshape(N_CTX, N_HEAD, 2 * ONE_ROWS, HEAD_DIM)[:, head].astype(F32)
    key = wide[:, :ONE_ROWS].reshape(GROUP_ROWS, HEAD_DIM).astype(BF16)
    value = wide[:, ONE_ROWS:].reshape(GROUP_ROWS, HEAD_DIM).astype(BF16)
    return key, value


def split_two(level_two, head):
    first = head * 2 * TWO_ROWS
    key = level_two[:, first : first + TWO_ROWS].reshape(LEVEL_TWO, HEAD_DIM)
    value = level_two[:, first + TWO_ROWS : first + 2 * TWO_ROWS].reshape(LEVEL_TWO, HEAD_DIM)
    return key, value


def near_bias(place, x):
    group, z = place[0], place[1]
    shape = (BLOCK, HEAD_DIM)
    low, high = jnp.zeros(shape, F32), jnp.zeros(shape, F32)
    if x == 0:
        low = jnp.full(shape, jnp.where((group == 0) & (z == 0), SHUT, 0.0).astype(F32))
    if x == N_X - 1:
        last = (group == N_GROUP - 1) & (z == N_Z - 1)
        high = jnp.full(shape, jnp.where(last, SHUT, 0.0).astype(F32))
    row = iota((GROUP_ROWS, HEAD_DIM), 0) // ONE_ROWS
    one = jnp.where(jnp.abs(row - (z * N_X + x)) <= 1, SHUT, 0.0).astype(F32)
    return [low, jnp.zeros(shape, F32), high, one]


def two_bias(place):
    row = iota((LEVEL_TWO, HEAD_DIM), 0) // TWO_ROWS
    return jnp.where(row == place[0], SHUT, 0.0).astype(F32)


def near_window(held, below, above, x, head, kind):
    rows = slice((1 + kind) * BLOCK, (2 + kind) * BLOCK)
    halo = slice(kind * BLOCK, (kind + 1) * BLOCK)
    unit = x * N_HEAD + head
    low = below[head, halo] if x == 0 else held[unit - N_HEAD, rows]
    high = above[head, halo] if x == N_X - 1 else held[unit + N_HEAD, rows]
    return [low, held[unit, rows], high]


def near_kernel(place, held, below, above, level_one, stats):
    for head in range(N_HEAD):
        one_k, one_v = split_one(level_one, head)
        for x in range(N_X):
            unit = x * N_HEAD + head
            all_k = jnp.concatenate(near_window(held, below, above, x, head, 0) + [one_k], axis=0)
            all_v = jnp.concatenate(near_window(held, below, above, x, head, 1) + [one_v], axis=0)
            bias = jnp.concatenate(near_bias(place, x), axis=0)
            scores = dot_nt(all_k, held[unit, QUERY]) * FACTOR + bias
            highest = jnp.max(scores, axis=0, keepdims=True)
            weights = jnp.exp(scores - highest)
            slopes = dot_nt(all_v, held[unit, COT])
            stats[unit, 0:1] = highest
            stats[unit, 1:2] = jnp.sum(weights, axis=0, keepdims=True)
            stats[unit, 2:3] = jnp.sum(weights * slopes, axis=0, keepdims=True)


def two_kernel(place, held, level_two, near, stats, part_two, chances, dscores):
    bias = two_bias(place)
    tokens = N_X * BLOCK
    for head in range(N_HEAD):
        key, value = split_two(level_two, head)
        for x in range(N_X):
            unit = x * N_HEAD + head
            scores = dot_nt(key, held[unit, QUERY]) * FACTOR + bias
            slopes = dot_nt(value, held[unit, COT])
            near_highest = near[unit, 0:1]
            highest = jnp.maximum(near_highest, jnp.max(scores, axis=0, keepdims=True))
            scale = jnp.exp(near_highest - highest)
            weights = jnp.exp(scores - highest)
            total = near[unit, 1:2] * scale + jnp.sum(weights, axis=0, keepdims=True)
            inverse = 1.0 / total
            centre = near[unit, 2:3] * scale + jnp.sum(weights * slopes, axis=0, keepdims=True)
            centre = centre * inverse
            stats[unit, 0:1] = highest
            stats[unit, 1:2] = inverse
            stats[unit, 2:3] = centre
            chance = weights * inverse
            dscores[head, :, lanes_of(x)] = (chance * (slopes - centre) * FACTOR).astype(BF16)
            chances[head, :, lanes_of(x)] = chance.astype(BF16)
        queries = jnp.concatenate([held[x * N_HEAD + head, QUERY] for x in range(N_X)], axis=0)
        cots = jnp.concatenate([held[x * N_HEAD + head, COT] for x in range(N_X)], axis=0)
        grad_k = dot_nn(dscores[head], queries).reshape(N_GROUP, TWO_ROWS, HEAD_DIM)
        grad_v = dot_nn(chances[head], cots).reshape(N_GROUP, TWO_ROWS, HEAD_DIM)
        rows = slice(head * 2 * TWO_ROWS, (head + 1) * 2 * TWO_ROWS)
        part_two[:, rows] = jnp.concatenate([grad_k, grad_v], axis=1).astype(BF16)


def attend_kernel(
    place, held, below, above, level_one, level_two, stats,
    result, grad_below, grad_above, part_one, window, ones,
):
    near = 3 * BLOCK
    seen = near + GROUP_ROWS
    shut = two_bias(place)
    for head in range(N_HEAD):
        one_k, one_v = split_one(level_one, head)
        two_k, two_v = split_two(level_two, head)
        window[head] = jnp.zeros_like(window[head])
        for x in range(N_X):
            unit = x * N_HEAD + head
            query, cot = held[unit, QUERY], held[unit, COT]
            near_k = near_window(held, below, above, x, head, 0)
            near_v = near_window(held, below, above, x, head, 1)
            all_k = jnp.concatenate(near_k + [one_k, two_k], axis=0)
            all_v = jnp.concatenate(near_v + [one_v, two_v], axis=0)
            bias = jnp.concatenate(near_bias(place, x) + [shut], axis=0)
            scores = dot_nt(all_k, query) * FACTOR + bias
            chance = jnp.exp(scores - stats[unit, 0:1]) * stats[unit, 1:2]
            slopes = dot_nt(all_v, cot)
            dscore = (chance * (slopes - stats[unit, 2:3]) * FACTOR).astype(BF16)
            chance = chance.astype(BF16)
            result[unit, :BLOCK] = dot_tn(chance, all_v).astype(BF16)
            result[unit, BLOCK : 2 * BLOCK] = dot_tn(dscore, all_k).astype(BF16)
            for kind, (left, right) in enumerate(((dscore, query), (chance, cot))):
                grad = dot_nn(left[:seen], right)
                window[head, kind, x * BLOCK : (x + 3) * BLOCK] += grad[:near]
                ones[head, kind] = grad[near:] if x == 0 else ones[head, kind] + grad[near:]
        for kind in range(2):
            rows = slice(kind * BLOCK, (kind + 1) * BLOCK)
            grad_below[head, rows] = window[head, kind, :BLOCK].astype(BF16)
            grad_above[head, rows] = window[head, kind, (N_X + 1) * BLOCK :].astype(BF16)
            fine = slice((2 + kind) * BLOCK, (3 + kind) * BLOCK)
            for x in range(N_X):
                own = window[head, kind, (x + 1) * BLOCK : (x + 2) * BLOCK]
                result[x * N_HEAD + head, fine] = own.astype(BF16)
        both = [ones[head, kind].reshape(N_CTX, ONE_ROWS, HEAD_DIM) for kind in range(2)]
        both = jnp.concatenate(both, axis=1)
        for ctx in range(N_CTX):
            first = ((ctx % N_X) * N_HEAD + head) * 2 * ONE_ROWS
            part_one[ctx // N_X, first : first + 2 * ONE_ROWS] = both[ctx]


def merge_kernel(part_one, arrived, merged):
    two = jnp.sum(arrived[...].astype(F32), axis=0) * 0.25
    for ctx in range(N_CTX):
        z, x = ctx // N_X, ctx % N_X
        for head in range(N_HEAD):
            low = head * 2 * TWO_ROWS + ctx // 2
            high = low + TWO_ROWS
            first = (x * N_HEAD + head) * 2 * ONE_ROWS
            rows = slice(first, first + 2 * ONE_ROWS)
            carried = jnp.concatenate(
                [
                    jnp.broadcast_to(two[low : low + 1], (ONE_ROWS, HEAD_DIM)),
                    jnp.broadcast_to(two[high : high + 1], (ONE_ROWS, HEAD_DIM)),
                ],
                axis=0,
            )
            merged[z, rows] = (part_one[z, rows] + carried).astype(BF16)


def edge_kernel(result, from_below, from_above, edged):
    edged[...] = result[...]
    for head in range(N_HEAD):
        for kind in range(2):
            rows = slice(kind * BLOCK, (kind + 1) * BLOCK)
            fine = slice((2 + kind) * BLOCK, (3 + kind) * BLOCK)
            for unit, arrived in ((head, from_below), (N_UNIT - N_HEAD + head, from_above)):
                grad = result[unit, fine].astype(F32) + arrived[head, rows].astype(F32)
                edged[unit, fine] = grad.astype(BF16)


def finish_kernel(edged, arrived, final):
    owned = jnp.sum(arrived[...].astype(F32), axis=0) * 0.25
    for unit in range(N_UNIT):
        final[unit, : 2 * BLOCK] = edged[unit, : 2 * BLOCK]
        for kind in range(2):
            fine = slice((2 + kind) * BLOCK, (3 + kind) * BLOCK)
            first = (2 * unit + kind) * ONE_ROWS
            carried = owned[first : first + ONE_ROWS].reshape(ONE_ROWS, 1, HEAD_DIM)
            total = edged[unit, fine].astype(F32).reshape(ONE_ROWS, COARSE, HEAD_DIM) + carried
            final[unit, fine] = total.reshape(BLOCK, HEAD_DIM).astype(BF16)


def unpack_kernel(packed, output, grad_q, grad_k, grad_v):
    for head in range(HEADS):
        for place, out in enumerate((output, grad_q, grad_k, grad_v)):
            out[:, lanes_of(head)] = packed[head, place * BLOCK : (place + 1) * BLOCK]


def shape_of(shape, dtype):
    return jax.ShapeDtypeStruct(shape, dtype)


def run(
    kernel, name, out_shape, *args, scratch=(), place=False, cost=None, limit=LIMIT
):
    several = isinstance(out_shape, tuple)
    specs = [SMEM if place and i == 0 else VMEM for i in range(len(args))]
    return pl.pallas_call(
        kernel,
        out_shape=out_shape,
        in_specs=specs,
        out_specs=(VMEM,) * len(out_shape) if several else VMEM,
        scratch_shapes=list(scratch),
        compiler_params=pltpu.CompilerParams(vmem_limit_bytes=limit),
        cost_estimate=cost,
        name=name,
    )(*args)


def shifted(value, steps):
    count = N_GROUP * N_Z
    first, last = max(0, -steps), min(count, count - steps)
    return lax.ppermute(value, LINE, [(s, s + steps) for s in range(first, last)])


def local(queries, keys, values, cotangent):
    group, z = lax.axis_index(GROUP), lax.axis_index("z")
    place = jnp.stack([group, z]).astype(jnp.int32)
    wide = (HEADS, 4 * BLOCK, HEAD_DIM)
    one = (N_Z, N_UNIT * 2 * ONE_ROWS, HEAD_DIM)
    two = (N_GROUP, N_HEAD * 2 * TWO_ROWS, HEAD_DIM)
    halo = (N_HEAD, 2 * BLOCK, HEAD_DIM)
    tokens = N_UNIT * BLOCK

    packed = run(pack_kernel, "pack", shape_of(wide, BF16), queries, keys, values, cotangent, limit=None)
    held = lax.all_to_all(packed, "x", 0, 0, tiled=True)

    spread = run(coarsen_one_kernel, "coarsen_one", shape_of(one, BF16), held)
    level_one = lax.all_to_all(spread, "z", 0, 0, tiled=True)
    below, above = shifted(held[-N_HEAD:, PAIR], 1), shifted(held[:N_HEAD, PAIR], -1)
    spread = run(coarsen_two_kernel, "coarsen_two", shape_of(two, BF16), level_one)
    level_two = lax.all_to_all(spread, GROUP, 0, 0, tiled=True)

    stats_shape = shape_of((N_UNIT, 8, HEAD_DIM), F32)
    near = run(
        near_kernel, "near_stats", stats_shape, place, held, below, above, level_one, place=True, cost=PHASE
    )
    stats, part_two = run(
        two_kernel, "level_two", (stats_shape, shape_of(two, BF16)),
        place, held, level_two, near, place=True,
        scratch=[pltpu.VMEM((N_HEAD, LEVEL_TWO, N_X * BLOCK), BF16)] * 2,
    )
    arrived_two = lax.all_to_all(part_two, GROUP, 0, 0, tiled=True)

    result, grad_below, grad_above, part_one = run(
        attend_kernel, "attend",
        (shape_of(wide, BF16), shape_of(halo, BF16), shape_of(halo, BF16), shape_of(one, F32)),
        place, held, below, above, level_one, level_two, stats, place=True, limit=2 * LIMIT,
        scratch=[
            pltpu.VMEM((N_HEAD, 2, (N_X + 2) * BLOCK, HEAD_DIM), F32),
            pltpu.VMEM((N_HEAD, 2, GROUP_ROWS, HEAD_DIM), F32),
        ],
        cost=pl.CostEstimate(
            flops=12 * tokens * 896 * HEAD_DIM, bytes_accessed=4 << 20, transcendentals=896 * tokens
        ),
    )
    merged = run(merge_kernel, "merge", shape_of(one, BF16), part_one, arrived_two)
    from_above = shifted(grad_below, -1)
    arrived_one = lax.all_to_all(merged, "z", 0, 0, tiled=True)
    from_below = shifted(grad_above, 1)
    edged = run(edge_kernel, "edge", shape_of(wide, BF16), result, from_below, from_above, cost=PHASE)
    result = run(finish_kernel, "finish", shape_of(wide, BF16), edged, arrived_one)
    arrived = lax.all_to_all(result, "x", 0, 0, tiled=True)
    outs = (shape_of((BLOCK, FEATURES), BF16),) * 4
    return run(unpack_kernel, "unpack", outs, arrived)


def solution(mesh):
    rows = Mesh(mesh.devices.reshape(N_Y, N_CORE, N_Z, N_X), AXES)
    placed = P(AXES, None)
    return jax.shard_map(
        local,
        mesh=rows,
        in_specs=(placed,) * 4,
        out_specs=(placed,) * 4,
        check_vma=False,
    )
```

```python
import jax
import jax.numpy as jnp
from jax import lax
from jax.experimental import pallas as pl
from jax.experimental.pallas import tpu as pltpu
from jax.sharding import Mesh
from jax.sharding import PartitionSpec as P

HEADS = 8
HEAD_DIM = 128
BLOCK = 128
COARSE = 16
ONE_ROWS = BLOCK // COARSE
N_Y, N_CORE, N_Z, N_X = 8, 2, 8, 4
AXES = ("y", "core", "z", "x")
GROUP = ("y", "core")
LINE = ("y", "core", "z")
N_HEAD = HEADS // N_X
N_UNIT = N_X * N_HEAD
N_CTX = N_Z * N_X
N_GROUP = N_Y * N_CORE
GROUP_ROWS = N_CTX * ONE_ROWS
TWO_ROWS = GROUP_ROWS // COARSE
LEVEL_TWO = N_GROUP * TWO_ROWS
FEATURES = HEADS * HEAD_DIM
FACTOR = HEAD_DIM ** (-0.5)
SHUT = -1e30
PHASE = pl.CostEstimate(flops=60_000_000_000, bytes_accessed=200 << 20, transcendentals=0)
LIMIT = 6 << 20
F32 = jnp.float32
BF16 = jnp.bfloat16
VMEM = pl.BlockSpec(memory_space=pltpu.VMEM)
SMEM = pl.BlockSpec(memory_space=pltpu.SMEM)
QUERY, KEY, VALUE, COT = (slice(i * BLOCK, (i + 1) * BLOCK) for i in range(4))
PAIR = slice(BLOCK, 3 * BLOCK)


def dot_nt(left, right):
    return lax.dot_general(left, right, (((1,), (1,)), ((), ())), preferred_element_type=F32)


def dot_nn(left, right):
    return lax.dot_general(left, right, (((1,), (0,)), ((), ())), preferred_element_type=F32)


def dot_tn(left, right):
    return lax.dot_general(left, right, (((0,), (0,)), ((), ())), preferred_element_type=F32)


def iota(shape, dim):
    return lax.broadcasted_iota(jnp.int32, shape, dim)


def lanes_of(head):
    return slice(head * HEAD_DIM, (head + 1) * HEAD_DIM)


def pack_kernel(queries, keys, values, cotangent, packed):
    for head in range(HEADS):
        for rows, source in ((QUERY, queries), (KEY, keys), (VALUE, values), (COT, cotangent)):
            packed[head, rows] = source[:, lanes_of(head)]


def coarsen_one_kernel(held, spread):
    row, token = iota((2 * ONE_ROWS, BLOCK), 0), iota((2 * ONE_ROWS, BLOCK), 1)
    pick_k = jnp.where(row == token // COARSE, 1.0, 0.0).astype(BF16)
    pick_v = jnp.where(row - ONE_ROWS == token // COARSE, 1.0, 0.0).astype(BF16)
    pick = jnp.concatenate([pick_k, pick_v], axis=1)
    for unit in range(N_UNIT):
        own = (dot_nn(pick, held[unit, PAIR]) * 0.25).astype(BF16)
        rows = slice(unit * 2 * ONE_ROWS, (unit + 1) * 2 * ONE_ROWS)
        for copy in range(N_Z):
            spread[copy, rows] = own


def coarsen_two_kernel(level_one, spread):
    width = N_UNIT * 2 * ONE_ROWS
    shape = (N_HEAD * 2 * TWO_ROWS, N_Z * width)
    row, source = iota(shape, 0), iota(shape, 1)
    z, rest = source // width, source % width
    unit, kind = rest // (2 * ONE_ROWS), (rest % (2 * ONE_ROWS)) // ONE_ROWS
    x, head = unit // N_HEAD, unit % N_HEAD
    target = (head * 2 + kind) * TWO_ROWS + (z * N_X + x) // 2
    pick = jnp.where(row == target, 1.0, 0.0).astype(BF16)
    own = dot_nn(pick, level_one[...].reshape(N_Z * width, HEAD_DIM))
    own = (own * 0.25).astype(BF16)
    for copy in range(N_GROUP):
        spread[copy] = own


def split_one(level_one, head):
    wide = level_one[...].reshape(N_CTX, N_HEAD, 2 * ONE_ROWS, HEAD_DIM)[:, head].astype(F32)
    key = wide[:, :ONE_ROWS].reshape(GROUP_ROWS, HEAD_DIM).astype(BF16)
    value = wide[:, ONE_ROWS:].reshape(GROUP_ROWS, HEAD_DIM).astype(BF16)
    return key, value


def split_two(level_two, head):
    first = head * 2 * TWO_ROWS
    key = level_two[:, first : first + TWO_ROWS].reshape(LEVEL_TWO, HEAD_DIM)
    value = level_two[:, first + TWO_ROWS : first + 2 * TWO_ROWS].reshape(LEVEL_TWO, HEAD_DIM)
    return key, value


def near_bias(place, x):
    group, z = place[0], place[1]
    shape = (BLOCK, HEAD_DIM)
    low, high = jnp.zeros(shape, F32), jnp.zeros(shape, F32)
    if x == 0:
        low = jnp.full(shape, jnp.where((group == 0) & (z == 0), SHUT, 0.0).astype(F32))
    if x == N_X - 1:
        last = (group == N_GROUP - 1) & (z == N_Z - 1)
        high = jnp.full(shape, jnp.where(last, SHUT, 0.0).astype(F32))
    row = iota((GROUP_ROWS, HEAD_DIM), 0) // ONE_ROWS
    one = jnp.where(jnp.abs(row - (z * N_X + x)) <= 1, SHUT, 0.0).astype(F32)
    return [low, jnp.zeros(shape, F32), high, one]


def two_bias(place):
    row = iota((LEVEL_TWO, HEAD_DIM), 0) // TWO_ROWS
    return jnp.where(row == place[0], SHUT, 0.0).astype(F32)


def near_window(held, below, above, x, head, kind):
    rows = slice((1 + kind) * BLOCK, (2 + kind) * BLOCK)
    halo = slice(kind * BLOCK, (kind + 1) * BLOCK)
    unit = x * N_HEAD + head
    low = below[head, halo] if x == 0 else held[unit - N_HEAD, rows]
    high = above[head, halo] if x == N_X - 1 else held[unit + N_HEAD, rows]
    return [low, held[unit, rows], high]


def near_kernel(place, held, below, above, level_one, stats):
    for head in range(N_HEAD):
        one_k, one_v = split_one(level_one, head)
        for x in range(N_X):
            unit = x * N_HEAD + head
            all_k = jnp.concatenate(near_window(held, below, above, x, head, 0) + [one_k], axis=0)
            all_v = jnp.concatenate(near_window(held, below, above, x, head, 1) + [one_v], axis=0)
            bias = jnp.concatenate(near_bias(place, x), axis=0)
            scores = dot_nt(all_k, held[unit, QUERY]) * FACTOR + bias
            highest = jnp.max(scores, axis=0, keepdims=True)
            weights = jnp.exp(scores - highest)
            slopes = dot_nt(all_v, held[unit, COT])
            stats[unit, 0:1] = highest
            stats[unit, 1:2] = jnp.sum(weights, axis=0, keepdims=True)
            stats[unit, 2:3] = jnp.sum(weights * slopes, axis=0, keepdims=True)


def two_kernel(place, held, level_two, near, stats, part_two, chances, dscores):
    bias = two_bias(place)
    tokens = N_X * BLOCK
    for head in range(N_HEAD):
        key, value = split_two(level_two, head)
        for x in range(N_X):
            unit = x * N_HEAD + head
            scores = dot_nt(key, held[unit, QUERY]) * FACTOR + bias
            slopes = dot_nt(value, held[unit, COT])
            near_highest = near[unit, 0:1]
            highest = jnp.maximum(near_highest, jnp.max(scores, axis=0, keepdims=True))
            scale = jnp.exp(near_highest - highest)
            weights = jnp.exp(scores - highest)
            total = near[unit, 1:2] * scale + jnp.sum(weights, axis=0, keepdims=True)
            inverse = 1.0 / total
            centre = near[unit, 2:3] * scale + jnp.sum(weights * slopes, axis=0, keepdims=True)
            centre = centre * inverse
            stats[unit, 0:1] = highest
            stats[unit, 1:2] = inverse
            stats[unit, 2:3] = centre
            chance = weights * inverse
            dscores[head, :, lanes_of(x)] = (chance * (slopes - centre) * FACTOR).astype(BF16)
            chances[head, :, lanes_of(x)] = chance.astype(BF16)
        queries = jnp.concatenate([held[x * N_HEAD + head, QUERY] for x in range(N_X)], axis=0)
        cots = jnp.concatenate([held[x * N_HEAD + head, COT] for x in range(N_X)], axis=0)
        grad_k = dot_nn(dscores[head], queries).reshape(N_GROUP, TWO_ROWS, HEAD_DIM)
        grad_v = dot_nn(chances[head], cots).reshape(N_GROUP, TWO_ROWS, HEAD_DIM)
        rows = slice(head * 2 * TWO_ROWS, (head + 1) * 2 * TWO_ROWS)
        part_two[:, rows] = jnp.concatenate([grad_k, grad_v], axis=1).astype(BF16)


def attend_kernel(
    place, held, below, above, level_one, level_two, stats,
    result, grad_below, grad_above, part_one, window, ones, total,
):
    near = 3 * BLOCK
    seen = near + GROUP_ROWS
    shut = two_bias(place)
    for head in range(N_HEAD):
        one_k, one_v = split_one(level_one, head)
        two_k, two_v = split_two(level_two, head)
        window[head] = jnp.zeros_like(window[head])
        for x in range(N_X):
            unit = x * N_HEAD + head
            query, cot = held[unit, QUERY], held[unit, COT]
            near_k = near_window(held, below, above, x, head, 0)
            near_v = near_window(held, below, above, x, head, 1)
            all_k = jnp.concatenate(near_k + [one_k, two_k], axis=0)
            all_v = jnp.concatenate(near_v + [one_v, two_v], axis=0)
            bias = jnp.concatenate(near_bias(place, x) + [shut], axis=0)
            scores = dot_nt(all_k, query) * FACTOR + bias
            chance = jnp.exp(scores - stats[unit, 0:1]) * stats[unit, 1:2]
            slopes = dot_nt(all_v, cot)
            dscore = (chance * (slopes - stats[unit, 2:3]) * FACTOR).astype(BF16)
            chance = chance.astype(BF16)
            total[unit, :BLOCK] = dot_tn(chance, all_v).astype(BF16)
            total[unit, BLOCK : 2 * BLOCK] = dot_tn(dscore, all_k).astype(BF16)
            for kind, (left, right) in enumerate(((dscore, query), (chance, cot))):
                grad = dot_nn(left[:seen], right)
                window[head, kind, x * BLOCK : (x + 3) * BLOCK] += grad[:near]
                ones[head, kind] = grad[near:] if x == 0 else ones[head, kind] + grad[near:]
        for kind in range(2):
            rows = slice(kind * BLOCK, (kind + 1) * BLOCK)
            grad_below[head, rows] = window[head, kind, :BLOCK].astype(BF16)
            grad_above[head, rows] = window[head, kind, (N_X + 1) * BLOCK :].astype(BF16)
            fine = slice((2 + kind) * BLOCK, (3 + kind) * BLOCK)
            for x in range(N_X):
                own = window[head, kind, (x + 1) * BLOCK : (x + 2) * BLOCK]
                total[x * N_HEAD + head, fine] = own.astype(BF16)
        both = [ones[head, kind].reshape(N_CTX, ONE_ROWS, HEAD_DIM) for kind in range(2)]
        both = jnp.concatenate(both, axis=1)
        for ctx in range(N_CTX):
            first = ((ctx % N_X) * N_HEAD + head) * 2 * ONE_ROWS
            part_one[ctx // N_X, first : first + 2 * ONE_ROWS] = both[ctx]
    result[...] = total[...]


def merge_kernel(part_one, arrived, merged):
    two = jnp.sum(arrived[...].astype(F32), axis=0) * 0.25
    for ctx in range(N_CTX):
        z, x = ctx // N_X, ctx % N_X
        for head in range(N_HEAD):
            low = head * 2 * TWO_ROWS + ctx // 2
            high = low + TWO_ROWS
            first = (x * N_HEAD + head) * 2 * ONE_ROWS
            rows = slice(first, first + 2 * ONE_ROWS)
            carried = jnp.concatenate(
                [
                    jnp.broadcast_to(two[low : low + 1], (ONE_ROWS, HEAD_DIM)),
                    jnp.broadcast_to(two[high : high + 1], (ONE_ROWS, HEAD_DIM)),
                ],
                axis=0,
            )
            merged[z, rows] = (part_one[z, rows] + carried).astype(BF16)


def edge_kernel(from_below, from_above, edge):
    edge[0] = from_below[...]
    edge[1] = from_above[...]


def finish_kernel(result, edge, arrived, final):
    owned = jnp.sum(arrived[...].astype(F32), axis=0) * 0.25
    for unit in range(N_UNIT):
        x, head = unit // N_HEAD, unit % N_HEAD
        final[unit, : 2 * BLOCK] = result[unit, : 2 * BLOCK]
        for kind in range(2):
            rows = slice(kind * BLOCK, (kind + 1) * BLOCK)
            fine = slice((2 + kind) * BLOCK, (3 + kind) * BLOCK)
            total = result[unit, fine].astype(F32)
            if x == 0:
                total = total + edge[0, head, rows].astype(F32)
            if x == N_X - 1:
                total = total + edge[1, head, rows].astype(F32)
            first = (2 * unit + kind) * ONE_ROWS
            carried = owned[first : first + ONE_ROWS].reshape(ONE_ROWS, 1, HEAD_DIM)
            total = total.reshape(ONE_ROWS, COARSE, HEAD_DIM) + carried
            final[unit, fine] = total.reshape(BLOCK, HEAD_DIM).astype(BF16)


def unpack_kernel(packed, output, grad_q, grad_k, grad_v):
    for head in range(HEADS):
        for place, out in enumerate((output, grad_q, grad_k, grad_v)):
            out[:, lanes_of(head)] = packed[head, place * BLOCK : (place + 1) * BLOCK]


def shape_of(shape, dtype):
    return jax.ShapeDtypeStruct(shape, dtype)


def run(
    kernel, name, out_shape, *args, scratch=(), place=False, cost=None, limit=LIMIT, aliases={}
):
    several = isinstance(out_shape, tuple)
    specs = [SMEM if place and i == 0 else VMEM for i in range(len(args))]
    return pl.pallas_call(
        kernel,
        out_shape=out_shape,
        in_specs=specs,
        out_specs=(VMEM,) * len(out_shape) if several else VMEM,
        scratch_shapes=list(scratch),
        compiler_params=pltpu.CompilerParams(vmem_limit_bytes=limit),
        cost_estimate=cost,
        input_output_aliases=aliases,
        name=name,
    )(*args)


def shifted(value, steps):
    count = N_GROUP * N_Z
    first, last = max(0, -steps), min(count, count - steps)
    return lax.ppermute(value, LINE, [(s, s + steps) for s in range(first, last)])


def local(queries, keys, values, cotangent):
    group, z = lax.axis_index(GROUP), lax.axis_index("z")
    place = jnp.stack([group, z]).astype(jnp.int32)
    wide = (HEADS, 4 * BLOCK, HEAD_DIM)
    one = (N_Z, N_UNIT * 2 * ONE_ROWS, HEAD_DIM)
    two = (N_GROUP, N_HEAD * 2 * TWO_ROWS, HEAD_DIM)
    halo = (N_HEAD, 2 * BLOCK, HEAD_DIM)
    tokens = N_UNIT * BLOCK

    packed = run(pack_kernel, "pack", shape_of(wide, BF16), queries, keys, values, cotangent, limit=None)
    held = lax.all_to_all(packed, "x", 0, 0, tiled=True)

    spread = run(coarsen_one_kernel, "coarsen_one", shape_of(one, BF16), held)
    level_one = lax.all_to_all(spread, "z", 0, 0, tiled=True)
    below, above = shifted(held[-N_HEAD:, PAIR], 1), shifted(held[:N_HEAD, PAIR], -1)
    spread = run(coarsen_two_kernel, "coarsen_two", shape_of(two, BF16), level_one)
    level_two = lax.all_to_all(spread, GROUP, 0, 0, tiled=True)

    stats_shape = shape_of((N_UNIT, 8, HEAD_DIM), F32)
    near = run(
        near_kernel, "near_stats", stats_shape, place, held, below, above, level_one, place=True, cost=PHASE
    )
    stats, part_two = run(
        two_kernel, "level_two", (stats_shape, shape_of(two, BF16)),
        place, held, level_two, near, place=True,
        scratch=[pltpu.VMEM((N_HEAD, LEVEL_TWO, N_X * BLOCK), BF16)] * 2,
    )
    arrived_two = lax.all_to_all(part_two, GROUP, 0, 0, tiled=True)

    result, grad_below, grad_above, part_one = run(
        attend_kernel, "attend",
        (shape_of(wide, BF16), shape_of(halo, BF16), shape_of(halo, BF16), shape_of(one, F32)),
        place, held, below, above, level_one, level_two, stats, place=True, limit=2 * LIMIT,
        scratch=[
            pltpu.VMEM((N_HEAD, 2, (N_X + 2) * BLOCK, HEAD_DIM), F32),
            pltpu.VMEM((N_HEAD, 2, GROUP_ROWS, HEAD_DIM), F32),
            pltpu.VMEM(wide, BF16),
        ],
        aliases={1: 0},
        cost=pl.CostEstimate(
            flops=12 * tokens * 896 * HEAD_DIM, bytes_accessed=4 << 20, transcendentals=896 * tokens
        ),
    )
    merged = run(merge_kernel, "merge", shape_of(one, BF16), part_one, arrived_two)
    from_above = shifted(grad_below, -1)
    arrived_one = lax.all_to_all(merged, "z", 0, 0, tiled=True)
    from_below = shifted(grad_above, 1)
    edge = run(edge_kernel, "edge", shape_of((2,) + halo, BF16), from_below, from_above, cost=PHASE)
    result = run(finish_kernel, "finish", shape_of(wide, BF16), result, edge, arrived_one)
    arrived = lax.all_to_all(result, "x", 0, 0, tiled=True)
    outs = (shape_of((BLOCK, FEATURES), BF16),) * 4
    return run(unpack_kernel, "unpack", outs, arrived)


def solution(mesh):
    rows = Mesh(mesh.devices.reshape(N_Y, N_CORE, N_Z, N_X), AXES)
    placed = P(AXES, None)
    return jax.shard_map(
        local,
        mesh=rows,
        in_specs=(placed,) * 4,
        out_specs=(placed,) * 4,
        check_vma=False,
    )
```

```python
import jax
import jax.numpy as jnp
from jax import lax
from jax.experimental import pallas as pl
from jax.experimental.pallas import tpu as pltpu
from jax.sharding import Mesh
from jax.sharding import PartitionSpec as P

HEADS = 8
HEAD_DIM = 128
BLOCK = 128
COARSE = 16
ONE_ROWS = BLOCK // COARSE
N_Y, N_CORE, N_Z, N_X = 8, 2, 4, 8
AXES = ("y", "core", "z", "x")
GROUP = ("y", "core")
LINE = ("y", "core", "z")
N_HEAD = HEADS // N_X
N_UNIT = N_X * N_HEAD
N_CTX = N_Z * N_X
N_GROUP = N_Y * N_CORE
GROUP_ROWS = N_CTX * ONE_ROWS
TWO_ROWS = GROUP_ROWS // COARSE
LEVEL_TWO = N_GROUP * TWO_ROWS
FEATURES = HEADS * HEAD_DIM
FACTOR = HEAD_DIM ** (-0.5)
SHUT = -1e30
PHASE = pl.CostEstimate(flops=60_000_000_000, bytes_accessed=200 << 20, transcendentals=0)
LIMIT = 6 << 20
F32 = jnp.float32
BF16 = jnp.bfloat16
VMEM = pl.BlockSpec(memory_space=pltpu.VMEM)
SMEM = pl.BlockSpec(memory_space=pltpu.SMEM)
QUERY, KEY, VALUE, COT = (slice(i * BLOCK, (i + 1) * BLOCK) for i in range(4))
PAIR = slice(BLOCK, 3 * BLOCK)


def dot_nt(left, right):
    return lax.dot_general(left, right, (((1,), (1,)), ((), ())), preferred_element_type=F32)


def dot_nn(left, right):
    return lax.dot_general(left, right, (((1,), (0,)), ((), ())), preferred_element_type=F32)


def dot_tn(left, right):
    return lax.dot_general(left, right, (((0,), (0,)), ((), ())), preferred_element_type=F32)


def iota(shape, dim):
    return lax.broadcasted_iota(jnp.int32, shape, dim)


def lanes_of(head):
    return slice(head * HEAD_DIM, (head + 1) * HEAD_DIM)


def pack_kernel(queries, keys, values, cotangent, packed):
    for head in range(HEADS):
        for rows, source in ((QUERY, queries), (KEY, keys), (VALUE, values), (COT, cotangent)):
            packed[head, rows] = source[:, lanes_of(head)]


def coarsen_one_kernel(held, spread):
    row, token = iota((2 * ONE_ROWS, BLOCK), 0), iota((2 * ONE_ROWS, BLOCK), 1)
    pick_k = jnp.where(row == token // COARSE, 1.0, 0.0).astype(BF16)
    pick_v = jnp.where(row - ONE_ROWS == token // COARSE, 1.0, 0.0).astype(BF16)
    pick = jnp.concatenate([pick_k, pick_v], axis=1)
    for unit in range(N_UNIT):
        own = (dot_nn(pick, held[unit, PAIR]) * 0.25).astype(BF16)
        rows = slice(unit * 2 * ONE_ROWS, (unit + 1) * 2 * ONE_ROWS)
        for copy in range(N_Z):
            spread[copy, rows] = own


def coarsen_two_kernel(level_one, spread):
    width = N_UNIT * 2 * ONE_ROWS
    shape = (N_HEAD * 2 * TWO_ROWS, N_Z * width)
    row, source = iota(shape, 0), iota(shape, 1)
    z, rest = source // width, source % width
    unit, kind = rest // (2 * ONE_ROWS), (rest % (2 * ONE_ROWS)) // ONE_ROWS
    x, head = unit // N_HEAD, unit % N_HEAD
    target = (head * 2 + kind) * TWO_ROWS + (z * N_X + x) // 2
    pick = jnp.where(row == target, 1.0, 0.0).astype(BF16)
    own = dot_nn(pick, level_one[...].reshape(N_Z * width, HEAD_DIM))
    own = (own * 0.25).astype(BF16)
    for copy in range(N_GROUP):
        spread[copy] = own


def split_one(level_one, head):
    wide = level_one[...].reshape(N_CTX, N_HEAD, 2 * ONE_ROWS, HEAD_DIM)[:, head].astype(F32)
    key = wide[:, :ONE_ROWS].reshape(GROUP_ROWS, HEAD_DIM).astype(BF16)
    value = wide[:, ONE_ROWS:].reshape(GROUP_ROWS, HEAD_DIM).astype(BF16)
    return key, value


def split_two(level_two, head):
    first = head * 2 * TWO_ROWS
    key = level_two[:, first : first + TWO_ROWS].reshape(LEVEL_TWO, HEAD_DIM)
    value = level_two[:, first + TWO_ROWS : first + 2 * TWO_ROWS].reshape(LEVEL_TWO, HEAD_DIM)
    return key, value


def near_bias(place, x):
    group, z = place[0], place[1]
    shape = (BLOCK, HEAD_DIM)
    low, high = jnp.zeros(shape, F32), jnp.zeros(shape, F32)
    if x == 0:
        low = jnp.full(shape, jnp.where((group == 0) & (z == 0), SHUT, 0.0).astype(F32))
    if x == N_X - 1:
        last = (group == N_GROUP - 1) & (z == N_Z - 1)
        high = jnp.full(shape, jnp.where(last, SHUT, 0.0).astype(F32))
    row = iota((GROUP_ROWS, HEAD_DIM), 0) // ONE_ROWS
    one = jnp.where(jnp.abs(row - (z * N_X + x)) <= 1, SHUT, 0.0).astype(F32)
    return [low, jnp.zeros(shape, F32), high, one]


def two_bias(place):
    row = iota((LEVEL_TWO, HEAD_DIM), 0) // TWO_ROWS
    return jnp.where(row == place[0], SHUT, 0.0).astype(F32)


def near_window(held, below, above, x, head, kind):
    rows = slice((1 + kind) * BLOCK, (2 + kind) * BLOCK)
    halo = slice(kind * BLOCK, (kind + 1) * BLOCK)
    unit = x * N_HEAD + head
    low = below[head, halo] if x == 0 else held[unit - N_HEAD, rows]
    high = above[head, halo] if x == N_X - 1 else held[unit + N_HEAD, rows]
    return [low, held[unit, rows], high]


def near_kernel(place, held, below, above, level_one, stats):
    for head in range(N_HEAD):
        one_k, one_v = split_one(level_one, head)
        for x in range(N_X):
            unit = x * N_HEAD + head
            all_k = jnp.concatenate(near_window(held, below, above, x, head, 0) + [one_k], axis=0)
            all_v = jnp.concatenate(near_window(held, below, above, x, head, 1) + [one_v], axis=0)
            bias = jnp.concatenate(near_bias(place, x), axis=0)
            scores = dot_nt(all_k, held[unit, QUERY]) * FACTOR + bias
            highest = jnp.max(scores, axis=0, keepdims=True)
            weights = jnp.exp(scores - highest)
            slopes = dot_nt(all_v, held[unit, COT])
            stats[unit, 0:1] = highest
            stats[unit, 1:2] = jnp.sum(weights, axis=0, keepdims=True)
            stats[unit, 2:3] = jnp.sum(weights * slopes, axis=0, keepdims=True)


def two_kernel(place, held, level_two, near, stats, part_two, chances, dscores):
    bias = two_bias(place)
    tokens = N_X * BLOCK
    for head in range(N_HEAD):
        key, value = split_two(level_two, head)
        for x in range(N_X):
            unit = x * N_HEAD + head
            scores = dot_nt(key, held[unit, QUERY]) * FACTOR + bias
            slopes = dot_nt(value, held[unit, COT])
            near_highest = near[unit, 0:1]
            highest = jnp.maximum(near_highest, jnp.max(scores, axis=0, keepdims=True))
            scale = jnp.exp(near_highest - highest)
            weights = jnp.exp(scores - highest)
            total = near[unit, 1:2] * scale + jnp.sum(weights, axis=0, keepdims=True)
            inverse = 1.0 / total
            centre = near[unit, 2:3] * scale + jnp.sum(weights * slopes, axis=0, keepdims=True)
            centre = centre * inverse
            stats[unit, 0:1] = highest
            stats[unit, 1:2] = inverse
            stats[unit, 2:3] = centre
            chance = weights * inverse
            dscores[head, :, lanes_of(x)] = (chance * (slopes - centre) * FACTOR).astype(BF16)
            chances[head, :, lanes_of(x)] = chance.astype(BF16)
        queries = jnp.concatenate([held[x * N_HEAD + head, QUERY] for x in range(N_X)], axis=0)
        cots = jnp.concatenate([held[x * N_HEAD + head, COT] for x in range(N_X)], axis=0)
        grad_k = dot_nn(dscores[head], queries).reshape(N_GROUP, TWO_ROWS, HEAD_DIM)
        grad_v = dot_nn(chances[head], cots).reshape(N_GROUP, TWO_ROWS, HEAD_DIM)
        rows = slice(head * 2 * TWO_ROWS, (head + 1) * 2 * TWO_ROWS)
        part_two[:, rows] = jnp.concatenate([grad_k, grad_v], axis=1).astype(BF16)


def attend_kernel(
    place, held, below, above, level_one, level_two, stats,
    result, grad_below, grad_above, part_one, window, ones, total,
):
    near = 3 * BLOCK
    seen = near + GROUP_ROWS
    shut = two_bias(place)
    for head in range(N_HEAD):
        one_k, one_v = split_one(level_one, head)
        two_k, two_v = split_two(level_two, head)
        window[head] = jnp.zeros_like(window[head])
        for x in range(N_X):
            unit = x * N_HEAD + head
            query, cot = held[unit, QUERY], held[unit, COT]
            near_k = near_window(held, below, above, x, head, 0)
            near_v = near_window(held, below, above, x, head, 1)
            all_k = jnp.concatenate(near_k + [one_k, two_k], axis=0)
            all_v = jnp.concatenate(near_v + [one_v, two_v], axis=0)
            bias = jnp.concatenate(near_bias(place, x) + [shut], axis=0)
            scores = dot_nt(all_k, query) * FACTOR + bias
            chance = jnp.exp(scores - stats[unit, 0:1]) * stats[unit, 1:2]
            slopes = dot_nt(all_v, cot)
            dscore = (chance * (slopes - stats[unit, 2:3]) * FACTOR).astype(BF16)
            chance = chance.astype(BF16)
            total[unit, :BLOCK] = dot_tn(chance, all_v).astype(BF16)
            total[unit, BLOCK : 2 * BLOCK] = dot_tn(dscore, all_k).astype(BF16)
            for kind, (left, right) in enumerate(((dscore, query), (chance, cot))):
                grad = dot_nn(left[:seen], right)
                window[head, kind, x * BLOCK : (x + 3) * BLOCK] += grad[:near]
                ones[head, kind] = grad[near:] if x == 0 else ones[head, kind] + grad[near:]
        for kind in range(2):
            rows = slice(kind * BLOCK, (kind + 1) * BLOCK)
            grad_below[head, rows] = window[head, kind, :BLOCK].astype(BF16)
            grad_above[head, rows] = window[head, kind, (N_X + 1) * BLOCK :].astype(BF16)
            fine = slice((2 + kind) * BLOCK, (3 + kind) * BLOCK)
            for x in range(N_X):
                own = window[head, kind, (x + 1) * BLOCK : (x + 2) * BLOCK]
                total[x * N_HEAD + head, fine] = own.astype(BF16)
        both = [ones[head, kind].reshape(N_CTX, ONE_ROWS, HEAD_DIM) for kind in range(2)]
        both = jnp.concatenate(both, axis=1)
        for ctx in range(N_CTX):
            first = ((ctx % N_X) * N_HEAD + head) * 2 * ONE_ROWS
            part_one[ctx // N_X, first : first + 2 * ONE_ROWS] = both[ctx]
    result[...] = total[...]


def merge_kernel(part_one, arrived, merged):
    two = jnp.sum(arrived[...].astype(F32), axis=0) * 0.25
    for ctx in range(N_CTX):
        z, x = ctx // N_X, ctx % N_X
        for head in range(N_HEAD):
            low = head * 2 * TWO_ROWS + ctx // 2
            high = low + TWO_ROWS
            first = (x * N_HEAD + head) * 2 * ONE_ROWS
            rows = slice(first, first + 2 * ONE_ROWS)
            carried = jnp.concatenate(
                [
                    jnp.broadcast_to(two[low : low + 1], (ONE_ROWS, HEAD_DIM)),
                    jnp.broadcast_to(two[high : high + 1], (ONE_ROWS, HEAD_DIM)),
                ],
                axis=0,
            )
            merged[z, rows] = (part_one[z, rows] + carried).astype(BF16)


def edge_kernel(from_below, from_above, edge):
    edge[0] = from_below[...]
    edge[1] = from_above[...]


def finish_kernel(result, edge, arrived, final):
    owned = jnp.sum(arrived[...].astype(F32), axis=0) * 0.25
    for unit in range(N_UNIT):
        x, head = unit // N_HEAD, unit % N_HEAD
        final[unit, : 2 * BLOCK] = result[unit, : 2 * BLOCK]
        for kind in range(2):
            rows = slice(kind * BLOCK, (kind + 1) * BLOCK)
            fine = slice((2 + kind) * BLOCK, (3 + kind) * BLOCK)
            total = result[unit, fine].astype(F32)
            if x == 0:
                total = total + edge[0, head, rows].astype(F32)
            if x == N_X - 1:
                total = total + edge[1, head, rows].astype(F32)
            first = (2 * unit + kind) * ONE_ROWS
            carried = owned[first : first + ONE_ROWS].reshape(ONE_ROWS, 1, HEAD_DIM)
            total = total.reshape(ONE_ROWS, COARSE, HEAD_DIM) + carried
            final[unit, fine] = total.reshape(BLOCK, HEAD_DIM).astype(BF16)


def unpack_kernel(packed, output, grad_q, grad_k, grad_v):
    for head in range(HEADS):
        for place, out in enumerate((output, grad_q, grad_k, grad_v)):
            out[:, lanes_of(head)] = packed[head, place * BLOCK : (place + 1) * BLOCK]


def shape_of(shape, dtype):
    return jax.ShapeDtypeStruct(shape, dtype)


def run(
    kernel, name, out_shape, *args, scratch=(), place=False, cost=None, limit=LIMIT, aliases={}
):
    several = isinstance(out_shape, tuple)
    specs = [SMEM if place and i == 0 else VMEM for i in range(len(args))]
    return pl.pallas_call(
        kernel,
        out_shape=out_shape,
        in_specs=specs,
        out_specs=(VMEM,) * len(out_shape) if several else VMEM,
        scratch_shapes=list(scratch),
        compiler_params=pltpu.CompilerParams(vmem_limit_bytes=limit),
        cost_estimate=cost,
        input_output_aliases=aliases,
        name=name,
    )(*args)


def shifted(value, steps):
    count = N_GROUP * N_Z
    first, last = max(0, -steps), min(count, count - steps)
    return lax.ppermute(value, LINE, [(s, s + steps) for s in range(first, last)])


def local(queries, keys, values, cotangent):
    group, z = lax.axis_index(GROUP), lax.axis_index("z")
    place = jnp.stack([group, z]).astype(jnp.int32)
    wide = (HEADS, 4 * BLOCK, HEAD_DIM)
    one = (N_Z, N_UNIT * 2 * ONE_ROWS, HEAD_DIM)
    two = (N_GROUP, N_HEAD * 2 * TWO_ROWS, HEAD_DIM)
    halo = (N_HEAD, 2 * BLOCK, HEAD_DIM)
    tokens = N_UNIT * BLOCK

    packed = run(pack_kernel, "pack", shape_of(wide, BF16), queries, keys, values, cotangent, limit=None)
    held = lax.all_to_all(packed, "x", 0, 0, tiled=True)

    spread = run(coarsen_one_kernel, "coarsen_one", shape_of(one, BF16), held)
    level_one = lax.all_to_all(spread, "z", 0, 0, tiled=True)
    below, above = shifted(held[-N_HEAD:, PAIR], 1), shifted(held[:N_HEAD, PAIR], -1)
    spread = run(coarsen_two_kernel, "coarsen_two", shape_of(two, BF16), level_one)
    level_two = lax.all_to_all(spread, GROUP, 0, 0, tiled=True)

    stats_shape = shape_of((N_UNIT, 8, HEAD_DIM), F32)
    near = run(
        near_kernel, "near_stats", stats_shape, place, held, below, above, level_one, place=True, cost=PHASE
    )
    stats, part_two = run(
        two_kernel, "level_two", (stats_shape, shape_of(two, BF16)),
        place, held, level_two, near, place=True,
        scratch=[pltpu.VMEM((N_HEAD, LEVEL_TWO, N_X * BLOCK), BF16)] * 2,
    )
    arrived_two = lax.all_to_all(part_two, GROUP, 0, 0, tiled=True)

    result, grad_below, grad_above, part_one = run(
        attend_kernel, "attend",
        (shape_of(wide, BF16), shape_of(halo, BF16), shape_of(halo, BF16), shape_of(one, F32)),
        place, held, below, above, level_one, level_two, stats, place=True, limit=2 * LIMIT,
        scratch=[
            pltpu.VMEM((N_HEAD, 2, (N_X + 2) * BLOCK, HEAD_DIM), F32),
            pltpu.VMEM((N_HEAD, 2, GROUP_ROWS, HEAD_DIM), F32),
            pltpu.VMEM(wide, BF16),
        ],
        aliases={1: 0},
        cost=pl.CostEstimate(
            flops=12 * tokens * 896 * HEAD_DIM, bytes_accessed=4 << 20, transcendentals=896 * tokens
        ),
    )
    merged = run(merge_kernel, "merge", shape_of(one, BF16), part_one, arrived_two)
    from_above = shifted(grad_below, -1)
    arrived_one = lax.all_to_all(merged, "z", 0, 0, tiled=True)
    from_below = shifted(grad_above, 1)
    edge = run(edge_kernel, "edge", shape_of((2,) + halo, BF16), from_below, from_above, cost=PHASE)
    result = run(finish_kernel, "finish", shape_of(wide, BF16), result, edge, arrived_one)
    arrived = lax.all_to_all(result, "x", 0, 0, tiled=True)
    outs = (shape_of((BLOCK, FEATURES), BF16),) * 4
    return run(unpack_kernel, "unpack", outs, arrived)


def solution(mesh):
    rows = Mesh(mesh.devices.reshape(N_Y, N_CORE, N_Z, N_X), AXES)
    placed = P(AXES, None)
    return jax.shard_map(
        local,
        mesh=rows,
        in_specs=(placed,) * 4,
        out_specs=(placed,) * 4,
        check_vma=False,
    )
```

```python
import jax
import jax.numpy as jnp
from jax import lax
from jax.experimental import pallas as pl
from jax.experimental.pallas import tpu as pltpu
from jax.sharding import Mesh
from jax.sharding import PartitionSpec as P

HEADS = 8
HEAD_DIM = 128
BLOCK = 128
COARSE = 16
ONE_ROWS = BLOCK // COARSE
N_Y, N_CORE, N_Z, N_X = 8, 2, 4, 8
AXES = ("y", "core", "z", "x")
GROUP = ("y", "core")
LINE = ("y", "core", "z")
N_HEAD = HEADS // N_X
N_UNIT = N_X * N_HEAD
N_CTX = N_Z * N_X
N_GROUP = N_Y * N_CORE
GROUP_ROWS = N_CTX * ONE_ROWS
TWO_ROWS = GROUP_ROWS // COARSE
LEVEL_TWO = N_GROUP * TWO_ROWS
FEATURES = HEADS * HEAD_DIM
FACTOR = HEAD_DIM ** (-0.5)
SHUT = -1e30
PHASE = pl.CostEstimate(flops=60_000_000_000, bytes_accessed=200 << 20, transcendentals=0)
LIMIT = 6 << 20
F32 = jnp.float32
BF16 = jnp.bfloat16
VMEM = pl.BlockSpec(memory_space=pltpu.VMEM)
SMEM = pl.BlockSpec(memory_space=pltpu.SMEM)
QUERY, KEY, VALUE, COT = (slice(i * BLOCK, (i + 1) * BLOCK) for i in range(4))
PAIR = slice(BLOCK, 3 * BLOCK)


def dot_nt(left, right):
    return lax.dot_general(left, right, (((1,), (1,)), ((), ())), preferred_element_type=F32)


def dot_nn(left, right):
    return lax.dot_general(left, right, (((1,), (0,)), ((), ())), preferred_element_type=F32)


def dot_tn(left, right):
    return lax.dot_general(left, right, (((0,), (0,)), ((), ())), preferred_element_type=F32)


def iota(shape, dim):
    return lax.broadcasted_iota(jnp.int32, shape, dim)


def lanes_of(head):
    return slice(head * HEAD_DIM, (head + 1) * HEAD_DIM)


def pack_kernel(queries, keys, values, cotangent, packed):
    for head in range(HEADS):
        for rows, source in ((QUERY, queries), (KEY, keys), (VALUE, values), (COT, cotangent)):
            packed[head, rows] = source[:, lanes_of(head)]


def coarsen_one_kernel(held, spread):
    row, token = iota((2 * ONE_ROWS, BLOCK), 0), iota((2 * ONE_ROWS, BLOCK), 1)
    pick_k = jnp.where(row == token // COARSE, 1.0, 0.0).astype(BF16)
    pick_v = jnp.where(row - ONE_ROWS == token // COARSE, 1.0, 0.0).astype(BF16)
    pick = jnp.concatenate([pick_k, pick_v], axis=1)
    for unit in range(N_UNIT):
        own = (dot_nn(pick, held[unit, PAIR]) * 0.25).astype(BF16)
        rows = slice(unit * 2 * ONE_ROWS, (unit + 1) * 2 * ONE_ROWS)
        for copy in range(N_Z):
            spread[copy, rows] = own


def coarsen_two_kernel(level_one, spread):
    width = N_UNIT * 2 * ONE_ROWS
    shape = (N_HEAD * 2 * TWO_ROWS, N_Z * width)
    row, source = iota(shape, 0), iota(shape, 1)
    z, rest = source // width, source % width
    unit, kind = rest // (2 * ONE_ROWS), (rest % (2 * ONE_ROWS)) // ONE_ROWS
    x, head = unit // N_HEAD, unit % N_HEAD
    target = (head * 2 + kind) * TWO_ROWS + (z * N_X + x) // 2
    pick = jnp.where(row == target, 1.0, 0.0).astype(BF16)
    own = dot_nn(pick, level_one[...].reshape(N_Z * width, HEAD_DIM))
    own = (own * 0.25).astype(BF16)
    for copy in range(N_GROUP):
        spread[copy] = own


def split_one(level_one, head):
    wide = level_one[...].reshape(N_CTX, N_HEAD, 2 * ONE_ROWS, HEAD_DIM)[:, head].astype(F32)
    key = wide[:, :ONE_ROWS].reshape(GROUP_ROWS, HEAD_DIM).astype(BF16)
    value = wide[:, ONE_ROWS:].reshape(GROUP_ROWS, HEAD_DIM).astype(BF16)
    return key, value


def split_two(level_two, head):
    first = head * 2 * TWO_ROWS
    key = level_two[:, first : first + TWO_ROWS].reshape(LEVEL_TWO, HEAD_DIM)
    value = level_two[:, first + TWO_ROWS : first + 2 * TWO_ROWS].reshape(LEVEL_TWO, HEAD_DIM)
    return key, value


def near_bias(place, x):
    group, z = place[0], place[1]
    shape = (BLOCK, HEAD_DIM)
    low, high = jnp.zeros(shape, F32), jnp.zeros(shape, F32)
    if x == 0:
        low = jnp.full(shape, jnp.where((group == 0) & (z == 0), SHUT, 0.0).astype(F32))
    if x == N_X - 1:
        last = (group == N_GROUP - 1) & (z == N_Z - 1)
        high = jnp.full(shape, jnp.where(last, SHUT, 0.0).astype(F32))
    row = iota((GROUP_ROWS, HEAD_DIM), 0) // ONE_ROWS
    one = jnp.where(jnp.abs(row - (z * N_X + x)) <= 1, SHUT, 0.0).astype(F32)
    return [low, jnp.zeros(shape, F32), high, one]


def two_bias(place):
    row = iota((LEVEL_TWO, HEAD_DIM), 0) // TWO_ROWS
    return jnp.where(row == place[0], SHUT, 0.0).astype(F32)


def near_window(held, below, above, x, head, kind):
    rows = slice((1 + kind) * BLOCK, (2 + kind) * BLOCK)
    halo = slice(kind * BLOCK, (kind + 1) * BLOCK)
    unit = x * N_HEAD + head
    low = below[head, halo] if x == 0 else held[unit - N_HEAD, rows]
    high = above[head, halo] if x == N_X - 1 else held[unit + N_HEAD, rows]
    return [low, held[unit, rows], high]


def near_kernel(place, held, below, above, level_one, stats):
    for head in range(N_HEAD):
        one_k, one_v = split_one(level_one, head)
        for x in range(N_X):
            unit = x * N_HEAD + head
            all_k = jnp.concatenate(near_window(held, below, above, x, head, 0) + [one_k], axis=0)
            all_v = jnp.concatenate(near_window(held, below, above, x, head, 1) + [one_v], axis=0)
            bias = jnp.concatenate(near_bias(place, x), axis=0)
            scores = dot_nt(all_k, held[unit, QUERY]) * FACTOR + bias
            highest = jnp.max(scores, axis=0, keepdims=True)
            weights = jnp.exp(scores - highest)
            slopes = dot_nt(all_v, held[unit, COT])
            stats[unit, 0:1] = highest
            stats[unit, 1:2] = jnp.sum(weights, axis=0, keepdims=True)
            stats[unit, 2:3] = jnp.sum(weights * slopes, axis=0, keepdims=True)


def two_kernel(place, held, level_two, near, stats, part_two, chances, dscores):
    bias = two_bias(place)
    tokens = N_X * BLOCK
    for head in range(N_HEAD):
        key, value = split_two(level_two, head)
        for x in range(N_X):
            unit = x * N_HEAD + head
            scores = dot_nt(key, held[unit, QUERY]) * FACTOR + bias
            slopes = dot_nt(value, held[unit, COT])
            near_highest = near[unit, 0:1]
            highest = jnp.maximum(near_highest, jnp.max(scores, axis=0, keepdims=True))
            scale = jnp.exp(near_highest - highest)
            weights = jnp.exp(scores - highest)
            total = near[unit, 1:2] * scale + jnp.sum(weights, axis=0, keepdims=True)
            inverse = 1.0 / total
            centre = near[unit, 2:3] * scale + jnp.sum(weights * slopes, axis=0, keepdims=True)
            centre = centre * inverse
            stats[unit, 0:1] = highest
            stats[unit, 1:2] = inverse
            stats[unit, 2:3] = centre
            chance = weights * inverse
            dscores[head, :, lanes_of(x)] = (chance * (slopes - centre) * FACTOR).astype(BF16)
            chances[head, :, lanes_of(x)] = chance.astype(BF16)
        queries = jnp.concatenate([held[x * N_HEAD + head, QUERY] for x in range(N_X)], axis=0)
        cots = jnp.concatenate([held[x * N_HEAD + head, COT] for x in range(N_X)], axis=0)
        grad_k = dot_nn(dscores[head], queries).reshape(N_GROUP, TWO_ROWS, HEAD_DIM)
        grad_v = dot_nn(chances[head], cots).reshape(N_GROUP, TWO_ROWS, HEAD_DIM)
        rows = slice(head * 2 * TWO_ROWS, (head + 1) * 2 * TWO_ROWS)
        part_two[:, rows] = jnp.concatenate([grad_k, grad_v], axis=1).astype(BF16)


def grads_kernel(
    place, held, below, above, level_one, stats,
    fine, grad_below, grad_above, part_one, window, ones,
):
    near = 3 * BLOCK
    for head in range(N_HEAD):
        one_k, one_v = split_one(level_one, head)
        window[head] = jnp.zeros_like(window[head])
        for x in range(N_X):
            unit = x * N_HEAD + head
            query, cot = held[unit, QUERY], held[unit, COT]
            all_k = jnp.concatenate(near_window(held, below, above, x, head, 0) + [one_k], axis=0)
            all_v = jnp.concatenate(near_window(held, below, above, x, head, 1) + [one_v], axis=0)
            bias = jnp.concatenate(near_bias(place, x), axis=0)
            scores = dot_nt(all_k, query) * FACTOR + bias
            chance = jnp.exp(scores - stats[unit, 0:1]) * stats[unit, 1:2]
            slopes = dot_nt(all_v, cot)
            dscore = (chance * (slopes - stats[unit, 2:3]) * FACTOR).astype(BF16)
            for kind, (left, right) in enumerate(((dscore, query), (chance.astype(BF16), cot))):
                grad = dot_nn(left, right)
                window[head, kind, x * BLOCK : (x + 3) * BLOCK] += grad[:near]
                ones[head, kind] = grad[near:] if x == 0 else ones[head, kind] + grad[near:]
        for kind in range(2):
            rows = slice(kind * BLOCK, (kind + 1) * BLOCK)
            grad_below[head, rows] = window[head, kind, :BLOCK].astype(BF16)
            grad_above[head, rows] = window[head, kind, (N_X + 1) * BLOCK :].astype(BF16)
            for x in range(N_X):
                own = window[head, kind, (x + 1) * BLOCK : (x + 2) * BLOCK]
                fine[x * N_HEAD + head, rows] = own.astype(BF16)
        both = [ones[head, kind].reshape(N_CTX, ONE_ROWS, HEAD_DIM) for kind in range(2)]
        both = jnp.concatenate(both, axis=1)
        for ctx in range(N_CTX):
            first = ((ctx % N_X) * N_HEAD + head) * 2 * ONE_ROWS
            part_one[ctx // N_X, first : first + 2 * ONE_ROWS] = both[ctx]


def answer_kernel(
    place, held, below, above, level_one, level_two, stats, fine, from_below, from_above,
    result, total,
):
    shut = two_bias(place)
    for head in range(N_HEAD):
        one_k, one_v = split_one(level_one, head)
        two_k, two_v = split_two(level_two, head)
        for x in range(N_X):
            unit = x * N_HEAD + head
            near_k = near_window(held, below, above, x, head, 0)
            near_v = near_window(held, below, above, x, head, 1)
            all_k = jnp.concatenate(near_k + [one_k, two_k], axis=0)
            all_v = jnp.concatenate(near_v + [one_v, two_v], axis=0)
            bias = jnp.concatenate(near_bias(place, x) + [shut], axis=0)
            scores = dot_nt(all_k, held[unit, QUERY]) * FACTOR + bias
            chance = jnp.exp(scores - stats[unit, 0:1]) * stats[unit, 1:2]
            slopes = dot_nt(all_v, held[unit, COT])
            dscore = (chance * (slopes - stats[unit, 2:3]) * FACTOR).astype(BF16)
            total[unit, :BLOCK] = dot_tn(chance.astype(BF16), all_v).astype(BF16)
            total[unit, BLOCK : 2 * BLOCK] = dot_tn(dscore, all_k).astype(BF16)
            total[unit, 2 * BLOCK :] = fine[unit]
        for unit, arrived in ((head, from_below), (N_UNIT - N_HEAD + head, from_above)):
            edge = fine[unit].astype(F32) + arrived[head].astype(F32)
            total[unit, 2 * BLOCK :] = edge.astype(BF16)
    result[...] = total[...]


def merge_kernel(part_one, arrived, merged):
    two = jnp.sum(arrived[...].astype(F32), axis=0) * 0.25
    for ctx in range(N_CTX):
        z, x = ctx // N_X, ctx % N_X
        for head in range(N_HEAD):
            low = head * 2 * TWO_ROWS + ctx // 2
            high = low + TWO_ROWS
            first = (x * N_HEAD + head) * 2 * ONE_ROWS
            rows = slice(first, first + 2 * ONE_ROWS)
            carried = jnp.concatenate(
                [
                    jnp.broadcast_to(two[low : low + 1], (ONE_ROWS, HEAD_DIM)),
                    jnp.broadcast_to(two[high : high + 1], (ONE_ROWS, HEAD_DIM)),
                ],
                axis=0,
            )
            merged[z, rows] = (part_one[z, rows] + carried).astype(BF16)


def finish_kernel(result, arrived, final):
    owned = jnp.sum(arrived[...].astype(F32), axis=0) * 0.25
    for unit in range(N_UNIT):
        final[unit, : 2 * BLOCK] = result[unit, : 2 * BLOCK]
        for kind in range(2):
            fine = slice((2 + kind) * BLOCK, (3 + kind) * BLOCK)
            total = result[unit, fine].astype(F32)
            first = (2 * unit + kind) * ONE_ROWS
            carried = owned[first : first + ONE_ROWS].reshape(ONE_ROWS, 1, HEAD_DIM)
            total = total.reshape(ONE_ROWS, COARSE, HEAD_DIM) + carried
            final[unit, fine] = total.reshape(BLOCK, HEAD_DIM).astype(BF16)


def unpack_kernel(packed, output, grad_q, grad_k, grad_v):
    for head in range(HEADS):
        for place, out in enumerate((output, grad_q, grad_k, grad_v)):
            out[:, lanes_of(head)] = packed[head, place * BLOCK : (place + 1) * BLOCK]


def shape_of(shape, dtype):
    return jax.ShapeDtypeStruct(shape, dtype)


def run(
    kernel, name, out_shape, *args, scratch=(), place=False, cost=None, limit=LIMIT, aliases={}
):
    several = isinstance(out_shape, tuple)
    specs = [SMEM if place and i == 0 else VMEM for i in range(len(args))]
    return pl.pallas_call(
        kernel,
        out_shape=out_shape,
        in_specs=specs,
        out_specs=(VMEM,) * len(out_shape) if several else VMEM,
        scratch_shapes=list(scratch),
        compiler_params=pltpu.CompilerParams(vmem_limit_bytes=limit),
        cost_estimate=cost,
        input_output_aliases=aliases,
        name=name,
    )(*args)


def shifted(value, steps):
    count = N_GROUP * N_Z
    first, last = max(0, -steps), min(count, count - steps)
    return lax.ppermute(value, LINE, [(s, s + steps) for s in range(first, last)])


def local(queries, keys, values, cotangent):
    group, z = lax.axis_index(GROUP), lax.axis_index("z")
    place = jnp.stack([group, z]).astype(jnp.int32)
    wide = (HEADS, 4 * BLOCK, HEAD_DIM)
    one = (N_Z, N_UNIT * 2 * ONE_ROWS, HEAD_DIM)
    two = (N_GROUP, N_HEAD * 2 * TWO_ROWS, HEAD_DIM)
    halo = (N_HEAD, 2 * BLOCK, HEAD_DIM)
    tokens = N_UNIT * BLOCK

    packed = run(pack_kernel, "pack", shape_of(wide, BF16), queries, keys, values, cotangent, limit=None)
    held = lax.all_to_all(packed, "x", 0, 0, tiled=True)

    spread = run(coarsen_one_kernel, "coarsen_one", shape_of(one, BF16), held)
    level_one = lax.all_to_all(spread, "z", 0, 0, tiled=True)
    below, above = shifted(held[-N_HEAD:, PAIR], 1), shifted(held[:N_HEAD, PAIR], -1)
    spread = run(coarsen_two_kernel, "coarsen_two", shape_of(two, BF16), level_one)
    level_two = lax.all_to_all(spread, GROUP, 0, 0, tiled=True)

    stats_shape = shape_of((N_UNIT, 8, HEAD_DIM), F32)
    near = run(
        near_kernel, "near_stats", stats_shape, place, held, below, above, level_one, place=True, cost=PHASE
    )
    stats, part_two = run(
        two_kernel, "level_two", (stats_shape, shape_of(two, BF16)),
        place, held, level_two, near, place=True,
        scratch=[pltpu.VMEM((N_HEAD, LEVEL_TWO, N_X * BLOCK), BF16)] * 2,
    )
    arrived_two = lax.all_to_all(part_two, GROUP, 0, 0, tiled=True)

    pair = shape_of((N_UNIT, 2 * BLOCK, HEAD_DIM), BF16)
    fine, grad_below, grad_above, part_one = run(
        grads_kernel, "grads", (pair, shape_of(halo, BF16), shape_of(halo, BF16), shape_of(one, F32)),
        place, held, below, above, level_one, stats, place=True, limit=2 * LIMIT,
        scratch=[
            pltpu.VMEM((N_HEAD, 2, (N_X + 2) * BLOCK, HEAD_DIM), F32),
            pltpu.VMEM((N_HEAD, 2, GROUP_ROWS, HEAD_DIM), F32),
        ],
        cost=pl.CostEstimate(
            flops=8 * tokens * 640 * HEAD_DIM, bytes_accessed=4 << 20, transcendentals=640 * tokens
        ),
    )
    from_above, from_below = shifted(grad_below, -1), shifted(grad_above, 1)
    merged = run(merge_kernel, "merge", shape_of(one, BF16), part_one, arrived_two)
    arrived_one = lax.all_to_all(merged, "z", 0, 0, tiled=True)
    result = run(
        answer_kernel, "answer", shape_of(wide, BF16),
        place, held, below, above, level_one, level_two, stats, fine, from_below, from_above,
        place=True, limit=2 * LIMIT, scratch=[pltpu.VMEM(wide, BF16)], aliases={1: 0}, cost=PHASE,
    )
    result = run(finish_kernel, "finish", shape_of(wide, BF16), result, arrived_one)
    arrived = lax.all_to_all(result, "x", 0, 0, tiled=True)
    outs = (shape_of((BLOCK, FEATURES), BF16),) * 4
    return run(unpack_kernel, "unpack", outs, arrived)


def solution(mesh):
    rows = Mesh(mesh.devices.reshape(N_Y, N_CORE, N_Z, N_X), AXES)
    placed = P(AXES, None)
    return jax.shard_map(
        local,
        mesh=rows,
        in_specs=(placed,) * 4,
        out_specs=(placed,) * 4,
        check_vma=False,
    )
```

```python
import jax
import jax.numpy as jnp
from jax import lax
from jax.experimental import pallas as pl
from jax.experimental.pallas import tpu as pltpu
from jax.sharding import Mesh
from jax.sharding import PartitionSpec as P

HEADS = 8
HEAD_DIM = 128
BLOCK = 128
COARSE = 16
ONE_ROWS = BLOCK // COARSE
N_Y, N_CORE, N_Z, N_X = 8, 2, 4, 8
AXES = ("y", "core", "z", "x")
GROUP = ("y", "core")
LINE = ("y", "core", "z")
N_HEAD = HEADS // N_X
N_UNIT = N_X * N_HEAD
N_CTX = N_Z * N_X
N_GROUP = N_Y * N_CORE
GROUP_ROWS = N_CTX * ONE_ROWS
TWO_ROWS = GROUP_ROWS // COARSE
LEVEL_TWO = N_GROUP * TWO_ROWS
FEATURES = HEADS * HEAD_DIM
FACTOR = HEAD_DIM ** (-0.5)
SHUT = -1e30
PHASE = pl.CostEstimate(flops=60_000_000_000, bytes_accessed=200 << 20, transcendentals=0)
LIMIT = 6 << 20
F32 = jnp.float32
BF16 = jnp.bfloat16
VMEM = pl.BlockSpec(memory_space=pltpu.VMEM)
SMEM = pl.BlockSpec(memory_space=pltpu.SMEM)
QUERY, KEY, VALUE, COT = (slice(i * BLOCK, (i + 1) * BLOCK) for i in range(4))
PAIR = slice(BLOCK, 3 * BLOCK)


def dot_nt(left, right):
    return lax.dot_general(left, right, (((1,), (1,)), ((), ())), preferred_element_type=F32)


def dot_nn(left, right):
    return lax.dot_general(left, right, (((1,), (0,)), ((), ())), preferred_element_type=F32)


def dot_tn(left, right):
    return lax.dot_general(left, right, (((0,), (0,)), ((), ())), preferred_element_type=F32)


def iota(shape, dim):
    return lax.broadcasted_iota(jnp.int32, shape, dim)


def lanes_of(head):
    return slice(head * HEAD_DIM, (head + 1) * HEAD_DIM)


def pack_kernel(queries, keys, values, cotangent, packed):
    for head in range(HEADS):
        for rows, source in ((QUERY, queries), (KEY, keys), (VALUE, values), (COT, cotangent)):
            packed[head, rows] = source[:, lanes_of(head)]


def coarsen_one_kernel(held, spread):
    row, token = iota((2 * ONE_ROWS, BLOCK), 0), iota((2 * ONE_ROWS, BLOCK), 1)
    pick_k = jnp.where(row == token // COARSE, 1.0, 0.0).astype(BF16)
    pick_v = jnp.where(row - ONE_ROWS == token // COARSE, 1.0, 0.0).astype(BF16)
    pick = jnp.concatenate([pick_k, pick_v], axis=1)
    for unit in range(N_UNIT):
        own = (dot_nn(pick, held[unit, PAIR]) * 0.25).astype(BF16)
        rows = slice(unit * 2 * ONE_ROWS, (unit + 1) * 2 * ONE_ROWS)
        for copy in range(N_Z):
            spread[copy, rows] = own


def coarsen_two_kernel(level_one, spread):
    width = N_UNIT * 2 * ONE_ROWS
    shape = (N_HEAD * 2 * TWO_ROWS, N_Z * width)
    row, source = iota(shape, 0), iota(shape, 1)
    z, rest = source // width, source % width
    unit, kind = rest // (2 * ONE_ROWS), (rest % (2 * ONE_ROWS)) // ONE_ROWS
    x, head = unit // N_HEAD, unit % N_HEAD
    target = (head * 2 + kind) * TWO_ROWS + (z * N_X + x) // 2
    pick = jnp.where(row == target, 1.0, 0.0).astype(BF16)
    own = dot_nn(pick, level_one[...].reshape(N_Z * width, HEAD_DIM))
    own = (own * 0.25).astype(BF16)
    for copy in range(N_GROUP):
        spread[copy] = own


def split_one(level_one, head):
    wide = level_one[...].reshape(N_CTX, N_HEAD, 2 * ONE_ROWS, HEAD_DIM)[:, head].astype(F32)
    key = wide[:, :ONE_ROWS].reshape(GROUP_ROWS, HEAD_DIM).astype(BF16)
    value = wide[:, ONE_ROWS:].reshape(GROUP_ROWS, HEAD_DIM).astype(BF16)
    return key, value


def split_two(level_two, head):
    first = head * 2 * TWO_ROWS
    key = level_two[:, first : first + TWO_ROWS].reshape(LEVEL_TWO, HEAD_DIM)
    value = level_two[:, first + TWO_ROWS : first + 2 * TWO_ROWS].reshape(LEVEL_TWO, HEAD_DIM)
    return key, value


def near_bias(place, x):
    group, z = place[0], place[1]
    shape = (BLOCK, HEAD_DIM)
    low, high = jnp.zeros(shape, F32), jnp.zeros(shape, F32)
    if x == 0:
        low = jnp.full(shape, jnp.where((group == 0) & (z == 0), SHUT, 0.0).astype(F32))
    if x == N_X - 1:
        last = (group == N_GROUP - 1) & (z == N_Z - 1)
        high = jnp.full(shape, jnp.where(last, SHUT, 0.0).astype(F32))
    row = iota((GROUP_ROWS, HEAD_DIM), 0) // ONE_ROWS
    one = jnp.where(jnp.abs(row - (z * N_X + x)) <= 1, SHUT, 0.0).astype(F32)
    return [low, jnp.zeros(shape, F32), high, one]


def two_bias(place):
    row = iota((LEVEL_TWO, HEAD_DIM), 0) // TWO_ROWS
    return jnp.where(row == place[0], SHUT, 0.0).astype(F32)


def near_window(held, below, above, x, head, kind):
    rows = slice((1 + kind) * BLOCK, (2 + kind) * BLOCK)
    halo = slice(kind * BLOCK, (kind + 1) * BLOCK)
    unit = x * N_HEAD + head
    low = below[head, halo] if x == 0 else held[unit - N_HEAD, rows]
    high = above[head, halo] if x == N_X - 1 else held[unit + N_HEAD, rows]
    return [low, held[unit, rows], high]


def near_kernel(place, held, below, above, level_one, stats):
    for head in range(N_HEAD):
        one_k, one_v = split_one(level_one, head)
        for x in range(N_X):
            unit = x * N_HEAD + head
            all_k = jnp.concatenate(near_window(held, below, above, x, head, 0) + [one_k], axis=0)
            all_v = jnp.concatenate(near_window(held, below, above, x, head, 1) + [one_v], axis=0)
            bias = jnp.concatenate(near_bias(place, x), axis=0)
            scores = dot_nt(all_k, held[unit, QUERY]) * FACTOR + bias
            highest = jnp.max(scores, axis=0, keepdims=True)
            weights = jnp.exp(scores - highest)
            slopes = dot_nt(all_v, held[unit, COT])
            stats[unit, 0:1] = highest
            stats[unit, 1:2] = jnp.sum(weights, axis=0, keepdims=True)
            stats[unit, 2:3] = jnp.sum(weights * slopes, axis=0, keepdims=True)


def two_kernel(place, held, level_two, near, stats, part_two, chances, dscores):
    bias = two_bias(place)
    tokens = N_X * BLOCK
    for head in range(N_HEAD):
        key, value = split_two(level_two, head)
        for x in range(N_X):
            unit = x * N_HEAD + head
            scores = dot_nt(key, held[unit, QUERY]) * FACTOR + bias
            slopes = dot_nt(value, held[unit, COT])
            near_highest = near[unit, 0:1]
            highest = jnp.maximum(near_highest, jnp.max(scores, axis=0, keepdims=True))
            scale = jnp.exp(near_highest - highest)
            weights = jnp.exp(scores - highest)
            total = near[unit, 1:2] * scale + jnp.sum(weights, axis=0, keepdims=True)
            inverse = 1.0 / total
            centre = near[unit, 2:3] * scale + jnp.sum(weights * slopes, axis=0, keepdims=True)
            centre = centre * inverse
            stats[unit, 0:1] = highest
            stats[unit, 1:2] = inverse
            stats[unit, 2:3] = centre
            chance = weights * inverse
            dscores[head, :, lanes_of(x)] = (chance * (slopes - centre) * FACTOR).astype(BF16)
            chances[head, :, lanes_of(x)] = chance.astype(BF16)
        queries = jnp.concatenate([held[x * N_HEAD + head, QUERY] for x in range(N_X)], axis=0)
        cots = jnp.concatenate([held[x * N_HEAD + head, COT] for x in range(N_X)], axis=0)
        grad_k = dot_nn(dscores[head], queries).reshape(N_GROUP, TWO_ROWS, HEAD_DIM)
        grad_v = dot_nn(chances[head], cots).reshape(N_GROUP, TWO_ROWS, HEAD_DIM)
        rows = slice(head * 2 * TWO_ROWS, (head + 1) * 2 * TWO_ROWS)
        part_two[:, rows] = jnp.concatenate([grad_k, grad_v], axis=1).astype(BF16)


def grads_kernel(
    place, held, below, above, level_one, stats,
    fine, grad_below, grad_above, part_one, window, ones,
):
    near = 3 * BLOCK
    for head in range(N_HEAD):
        one_k, one_v = split_one(level_one, head)
        window[head] = jnp.zeros_like(window[head])
        for x in range(N_X):
            unit = x * N_HEAD + head
            query, cot = held[unit, QUERY], held[unit, COT]
            all_k = jnp.concatenate(near_window(held, below, above, x, head, 0) + [one_k], axis=0)
            all_v = jnp.concatenate(near_window(held, below, above, x, head, 1) + [one_v], axis=0)
            bias = jnp.concatenate(near_bias(place, x), axis=0)
            scores = dot_nt(all_k, query) * FACTOR + bias
            chance = jnp.exp(scores - stats[unit, 0:1]) * stats[unit, 1:2]
            slopes = dot_nt(all_v, cot)
            dscore = (chance * (slopes - stats[unit, 2:3]) * FACTOR).astype(BF16)
            for kind, (left, right) in enumerate(((dscore, query), (chance.astype(BF16), cot))):
                grad = dot_nn(left, right)
                window[head, kind, x * BLOCK : (x + 3) * BLOCK] += grad[:near]
                ones[head, kind] = grad[near:] if x == 0 else ones[head, kind] + grad[near:]
        for kind in range(2):
            rows = slice(kind * BLOCK, (kind + 1) * BLOCK)
            grad_below[head, rows] = window[head, kind, :BLOCK].astype(BF16)
            grad_above[head, rows] = window[head, kind, (N_X + 1) * BLOCK :].astype(BF16)
            for x in range(N_X):
                own = window[head, kind, (x + 1) * BLOCK : (x + 2) * BLOCK]
                fine[x * N_HEAD + head, rows] = own.astype(BF16)
        both = [ones[head, kind].reshape(N_CTX, ONE_ROWS, HEAD_DIM) for kind in range(2)]
        both = jnp.concatenate(both, axis=1)
        for ctx in range(N_CTX):
            first = ((ctx % N_X) * N_HEAD + head) * 2 * ONE_ROWS
            part_one[ctx // N_X, first : first + 2 * ONE_ROWS] = both[ctx]


def answer_kernel(
    place, held, below, above, level_one, level_two, stats, fine, from_below, from_above,
    result, total,
):
    shut = two_bias(place)
    for head in range(N_HEAD):
        one_k, one_v = split_one(level_one, head)
        two_k, two_v = split_two(level_two, head)
        for x in range(N_X):
            unit = x * N_HEAD + head
            near_k = near_window(held, below, above, x, head, 0)
            near_v = near_window(held, below, above, x, head, 1)
            all_k = jnp.concatenate(near_k + [one_k, two_k], axis=0)
            all_v = jnp.concatenate(near_v + [one_v, two_v], axis=0)
            bias = jnp.concatenate(near_bias(place, x) + [shut], axis=0)
            scores = dot_nt(all_k, held[unit, QUERY]) * FACTOR + bias
            chance = jnp.exp(scores - stats[unit, 0:1]) * stats[unit, 1:2]
            slopes = dot_nt(all_v, held[unit, COT])
            dscore = (chance * (slopes - stats[unit, 2:3]) * FACTOR).astype(BF16)
            total[unit, :BLOCK] = dot_tn(chance.astype(BF16), all_v).astype(BF16)
            total[unit, BLOCK : 2 * BLOCK] = dot_tn(dscore, all_k).astype(BF16)
            total[unit, 2 * BLOCK :] = fine[unit]
        for unit, arrived in ((head, from_below), (N_UNIT - N_HEAD + head, from_above)):
            edge = fine[unit].astype(F32) + arrived[head].astype(F32)
            total[unit, 2 * BLOCK :] = edge.astype(BF16)
    result[...] = total[...]


def merge_kernel(part_one, arrived, merged):
    two = jnp.sum(arrived[...].astype(F32), axis=0) * 0.25
    for ctx in range(N_CTX):
        z, x = ctx // N_X, ctx % N_X
        for head in range(N_HEAD):
            low = head * 2 * TWO_ROWS + ctx // 2
            high = low + TWO_ROWS
            first = (x * N_HEAD + head) * 2 * ONE_ROWS
            rows = slice(first, first + 2 * ONE_ROWS)
            carried = jnp.concatenate(
                [
                    jnp.broadcast_to(two[low : low + 1], (ONE_ROWS, HEAD_DIM)),
                    jnp.broadcast_to(two[high : high + 1], (ONE_ROWS, HEAD_DIM)),
                ],
                axis=0,
            )
            merged[z, rows] = (part_one[z, rows] + carried).astype(BF16)


def finish_kernel(result, arrived, final):
    owned = jnp.sum(arrived[...].astype(F32), axis=0) * 0.25
    for unit in range(N_UNIT):
        final[unit, : 2 * BLOCK] = result[unit, : 2 * BLOCK]
        for kind in range(2):
            fine = slice((2 + kind) * BLOCK, (3 + kind) * BLOCK)
            total = result[unit, fine].astype(F32)
            first = (2 * unit + kind) * ONE_ROWS
            carried = owned[first : first + ONE_ROWS].reshape(ONE_ROWS, 1, HEAD_DIM)
            total = total.reshape(ONE_ROWS, COARSE, HEAD_DIM) + carried
            final[unit, fine] = total.reshape(BLOCK, HEAD_DIM).astype(BF16)


def unpack_kernel(packed, output, grad_q, grad_k, grad_v):
    for head in range(HEADS):
        for place, out in enumerate((output, grad_q, grad_k, grad_v)):
            out[:, lanes_of(head)] = packed[head, place * BLOCK : (place + 1) * BLOCK]


def shape_of(shape, dtype):
    return jax.ShapeDtypeStruct(shape, dtype)


def run(
    kernel, name, out_shape, *args, scratch=(), place=False, cost=None, limit=LIMIT, aliases={}
):
    several = isinstance(out_shape, tuple)
    specs = [SMEM if place and i == 0 else VMEM for i in range(len(args))]
    return pl.pallas_call(
        kernel,
        out_shape=out_shape,
        in_specs=specs,
        out_specs=(VMEM,) * len(out_shape) if several else VMEM,
        scratch_shapes=list(scratch),
        compiler_params=pltpu.CompilerParams(vmem_limit_bytes=limit),
        cost_estimate=cost,
        input_output_aliases=aliases,
        name=name,
    )(*args)


def shifted(value, steps):
    count = N_GROUP * N_Z
    first, last = max(0, -steps), min(count, count - steps)
    return lax.ppermute(value, LINE, [(s, s + steps) for s in range(first, last)])


def local(queries, keys, values, cotangent):
    group, z = lax.axis_index(GROUP), lax.axis_index("z")
    place = jnp.stack([group, z]).astype(jnp.int32)
    wide = (HEADS, 4 * BLOCK, HEAD_DIM)
    one = (N_Z, N_UNIT * 2 * ONE_ROWS, HEAD_DIM)
    two = (N_GROUP, N_HEAD * 2 * TWO_ROWS, HEAD_DIM)
    halo = (N_HEAD, 2 * BLOCK, HEAD_DIM)
    tokens = N_UNIT * BLOCK

    packed = run(pack_kernel, "pack", shape_of(wide, BF16), queries, keys, values, cotangent, limit=None)
    held = lax.all_to_all(packed, "x", 0, 0, tiled=True)

    spread = run(coarsen_one_kernel, "coarsen_one", shape_of(one, BF16), held)
    level_one = lax.all_to_all(spread, "z", 0, 0, tiled=True)
    below, above = shifted(held[-N_HEAD:, PAIR], 1), shifted(held[:N_HEAD, PAIR], -1)
    spread = run(coarsen_two_kernel, "coarsen_two", shape_of(two, BF16), level_one)
    level_two = lax.all_to_all(spread, GROUP, 0, 0, tiled=True)

    stats_shape = shape_of((N_UNIT, 8, HEAD_DIM), F32)
    near = run(
        near_kernel, "near_stats", stats_shape, place, held, below, above, level_one, place=True
    )
    stats, part_two = run(
        two_kernel, "level_two", (stats_shape, shape_of(two, BF16)),
        place, held, level_two, near, place=True,
        scratch=[pltpu.VMEM((N_HEAD, LEVEL_TWO, N_X * BLOCK), BF16)] * 2,
    )
    arrived_two = lax.all_to_all(part_two, GROUP, 0, 0, tiled=True)

    pair = shape_of((N_UNIT, 2 * BLOCK, HEAD_DIM), BF16)
    fine, grad_below, grad_above, part_one = run(
        grads_kernel, "grads", (pair, shape_of(halo, BF16), shape_of(halo, BF16), shape_of(one, F32)),
        place, held, below, above, level_one, stats, place=True, limit=2 * LIMIT,
        scratch=[
            pltpu.VMEM((N_HEAD, 2, (N_X + 2) * BLOCK, HEAD_DIM), F32),
            pltpu.VMEM((N_HEAD, 2, GROUP_ROWS, HEAD_DIM), F32),
        ],
        cost=pl.CostEstimate(
            flops=8 * tokens * 640 * HEAD_DIM, bytes_accessed=4 << 20, transcendentals=640 * tokens
        ),
    )
    from_above, from_below = shifted(grad_below, -1), shifted(grad_above, 1)
    merged = run(merge_kernel, "merge", shape_of(one, BF16), part_one, arrived_two)
    arrived_one = lax.all_to_all(merged, "z", 0, 0, tiled=True)
    result = run(
        answer_kernel, "answer", shape_of(wide, BF16),
        place, held, below, above, level_one, level_two, stats, fine, from_below, from_above,
        place=True, limit=2 * LIMIT, scratch=[pltpu.VMEM(wide, BF16)], aliases={1: 0}, cost=PHASE,
    )
    result = run(finish_kernel, "finish", shape_of(wide, BF16), result, arrived_one)
    arrived = lax.all_to_all(result, "x", 0, 0, tiled=True)
    outs = (shape_of((BLOCK, FEATURES), BF16),) * 4
    return run(unpack_kernel, "unpack", outs, arrived)


def solution(mesh):
    rows = Mesh(mesh.devices.reshape(N_Y, N_CORE, N_Z, N_X), AXES)
    placed = P(AXES, None)
    return jax.shard_map(
        local,
        mesh=rows,
        in_specs=(placed,) * 4,
        out_specs=(placed,) * 4,
        check_vma=False,
    )
```
